128 devices in a mesh: dp: 4 (over z), feat: 32 (over y, x, core).
Axes of the slice: x: 4, y: 4, z: 4, core: 2. Of those that a mesh axis runs over, the one named last changes fastest.
Arguments:
- features: bfloat16 [1024, 16384], P('feat'), may hold values from -6 to 6
- targets: int32 [4, 4096], P('dp'), may hold values from 0 to 16383
- block_ids: int32 [4, 32, 16], P('dp'), may hold values from 0 to 127
- counts: int32 [4, 32], P('dp'), may hold values from 1 to 16, as said below
- target_slots: int32 [4, 4096], P('dp'), may hold values from 0 to 4095, each once within a row
- edge_tiles: bfloat16 [4, 32, 16, 128, 128], P('dp'), may hold values from -0.125 to 0.125
- self_weight: bfloat16 [1024, 256], P('feat'), may hold values from -0.1875 to 0.1875
- neigh_weight: bfloat16 [1024, 256], P('feat'), may hold values from -0.1875 to 0.1875
- hidden_bias: float32 [256], replicated, may hold values from -3 to 3
- hidden_grad: bfloat16 [4, 4096, 256], P('dp', 'feat'), may hold values from -6 to 6
Outputs:
- hidden: bfloat16 [4, 4096, 256], P('dp', 'feat')
- feature_grad: float32 [1024, 16384], P('feat')
- self_weight_grad: float32 [1024, 256], P('feat')
- neigh_weight_grad: float32 [1024, 256], P('feat')
- bias_grad: float32 [256], replicated
The draws below stay inside these ranges and needn't reach their ends.
Inputs may be any that keep to these rules, and one draw needn't show every extreme that they name: `counts`: every group has a target block with 16 live slots and one with a single live slot.
All inputs are finite; a program needn't handle non-finite values.
Results may differ from the reference program's by a relative error of at most 0.0052.
Values may be sent and summed in bfloat16 or wider, within the bound.
No kernel may reach another device: no remote copies, remote signals or barrier semaphores. Data moves between devices by JAX's collectives and lax.ppermute only.
A program may use at most 128 MiB of HBM per device.

```python
import jax
import jax.numpy as jnp
from jax import lax

D = 1024
H = 256
BLK = 128
MAXB = 16
TB = 32
NBLK = 128
TGT = 4096
NODES = 16384
N_DP = 4


def draw_counts(key, part):
    key = jax.random.fold_in(key, 7)
    raw = jax.random.randint(key, (N_DP, TB), 0, MAXB + 1)
    filled = jnp.minimum(1 + raw * raw // MAXB, MAXB)
    filled = filled.at[:, 0].set(MAXB)
    filled = filled.at[:, TB - 1].set(1)
    return filled.astype(jnp.int32)


def place_ends(drawn, stream_key, least, top_value):
    longest = drawn.shape.index(max(drawn.shape))
    spots = []
    for shift in (0, 1):
        where = [jax.random.randint(jax.random.fold_in(stream_key, axis), (), 0, length) for axis, length in enumerate(drawn.shape)]
        where[longest] = (where[longest] + shift) % drawn.shape[longest]
        spots.append(tuple(where))
    return drawn.at[spots[0]].set(least).at[spots[1]].set(top_value)


def levels(stream_key, shape, shards, smallest, high):
    loudness, own = 1.0, jax.random.fold_in(stream_key, 6)
    for position, parts in shards:
        heights = jnp.exp(jax.random.uniform(jax.random.fold_in(own, position), (parts,), jnp.float32, smallest / len(shards), high / len(shards)))
        loudness = loudness * jnp.repeat(heights, shape[position] // parts).reshape([-1 if axis == position else 1 for axis in range(len(shape))])
    return loudness


def normal_values(key, shape, scale, reach, pieces=(), held_as=jnp.bfloat16):
    factor_of = levels(key, shape, pieces, -0.22, 0.18) if pieces else 1.0
    values = jax.random.normal(key, shape, jnp.float32) * scale * factor_of
    return jnp.minimum(jnp.maximum(values, -reach), reach).astype(held_as)


def setup_inputs(seed: int = 0) -> dict:
    seeds = jax.random.split(jax.random.key(seed), 11)
    return {
        "features": normal_values(seeds[0], (D, NODES), 1.0, 6.0, ((0, 32),)),
        "targets": place_ends(jax.random.randint(seeds[1], (N_DP, TGT), 0, NODES), jax.random.fold_in(seeds[1], 1), 0, NODES - 1).astype(jnp.int32),
        "block_ids": place_ends(jax.random.randint(seeds[2], (N_DP, TB, MAXB), 0, NBLK), jax.random.fold_in(seeds[2], 1), 0, NBLK - 1).astype(jnp.int32),
        "counts": draw_counts(jax.random.fold_in(seeds[10], 71), 0),
        "target_slots": jax.vmap(lambda own: jax.random.permutation(own, TGT))(jax.random.split(seeds[4], N_DP)).reshape((N_DP, TGT)).astype(jnp.int32),
        "edge_tiles": normal_values(seeds[5], (N_DP, TB, MAXB, BLK, BLK), (BLK * MAXB) ** -0.5, 0.125, ((0, 4),)),
        "self_weight": normal_values(seeds[6], (D, H), D ** -0.5, 0.1875, ((0, 32),)),
        "neigh_weight": normal_values(seeds[7], (D, H), D ** -0.5, 0.1875, ((0, 32),)),
        "hidden_bias": normal_values(seeds[8], (H,), 0.5, 3.0, (), jnp.float32),
        "hidden_grad": normal_values(seeds[9], (N_DP, TGT, H), 1.0, 6.0, ((0, 4), (1, 32))),
    }


def product(left, right, dims):
    return lax.dot_general(left.astype(jnp.float32), right.astype(jnp.float32), (dims, ((), ())), precision=lax.Precision.HIGHEST, preferred_element_type=jnp.float32)


def member_pass(features, targets, block_ids, counts, target_slots, edge_tiles, self_weight, neigh_weight, hidden_bias, hidden_grad):
    width = features.shape[0]
    node_blocks = features.reshape(width, NBLK, BLK)
    live = (jnp.arange(MAXB, dtype=jnp.int32)[None, :] < counts[:, None]).astype(jnp.float32)
    gathered = jnp.take(node_blocks, block_ids.reshape(-1), axis=1).reshape(width, TB, MAXB, BLK).astype(jnp.float32)
    gathered = gathered * live[None, :, :, None]
    tiles_wide = edge_tiles.astype(jnp.float32)
    aggregate = jnp.einsum("cbjs,bjst->cbt", gathered, tiles_wide, precision=lax.Precision.HIGHEST).reshape(width, TGT).astype(jnp.bfloat16)
    own = jnp.take(features, targets, axis=1)
    preact = product(own, self_weight, ((0,), (0,))) + product(aggregate, neigh_weight, ((0,), (0,))) + hidden_bias
    sigmoid_val = jax.nn.sigmoid(preact)
    activated = (preact * sigmoid_val).astype(jnp.bfloat16)
    hidden = jnp.zeros((TGT, activated.shape[1]), jnp.bfloat16).at[target_slots].set(activated)
    grad_rows = jnp.take(hidden_grad, target_slots, axis=0).astype(jnp.float32)
    slope = (grad_rows * sigmoid_val * (1.0 + preact * (1.0 - sigmoid_val))).astype(jnp.bfloat16)
    self_grad = product(own, slope, ((1,), (0,)))
    neigh_grad = product(aggregate, slope, ((1,), (0,)))
    bias_grad = jnp.sum(slope.astype(jnp.float32), axis=0)
    own_back = product(self_weight, slope, ((1,), (1,))).astype(jnp.bfloat16)
    aggregate_back = product(neigh_weight, slope, ((1,), (1,))).astype(jnp.bfloat16)
    spread = jnp.einsum("cbt,bjst->cbjs", aggregate_back.reshape(width, TB, BLK).astype(jnp.float32), tiles_wide, precision=lax.Precision.HIGHEST)
    spread = spread * live[None, :, :, None]
    feature_grad = jnp.zeros((width, NBLK, BLK), jnp.float32).at[:, block_ids.reshape(-1)].add(spread.reshape(width, TB * MAXB, BLK))
    feature_grad = feature_grad.reshape(width, NODES).at[:, targets].add(own_back.astype(jnp.float32))
    return hidden, feature_grad, self_grad, neigh_grad, bias_grad


def reference(features, targets, block_ids, counts, target_slots, edge_tiles, self_weight, neigh_weight, hidden_bias, hidden_grad):
    hidden_list = []
    feature_grad = jnp.zeros(features.shape, jnp.float32)
    self_grad = jnp.zeros(self_weight.shape, jnp.float32)
    neigh_grad = jnp.zeros(neigh_weight.shape, jnp.float32)
    bias_grad = jnp.zeros(hidden_bias.shape, jnp.float32)
    for member in range(N_DP):
        results = member_pass(features, targets[member], block_ids[member], counts[member], target_slots[member], edge_tiles[member], self_weight, neigh_weight, hidden_bias, hidden_grad[member])
        hidden_list.append(results[0])
        feature_grad = feature_grad + results[1]
        self_grad = self_grad + results[2]
        neigh_grad = neigh_grad + results[3]
        bias_grad = bias_grad + results[4]
    return jnp.stack(hidden_list), feature_grad, self_grad, neigh_grad, bias_grad
```

```python
import jax
import jax.numpy as jnp
from jax import lax
from jax.experimental import pallas as pl
from jax.experimental.pallas import tpu as pltpu
from jax.sharding import PartitionSpec as P

BLK = 128
MAXB = 16
TB = 32
NBLK = 128
TGT = 4096
NODES = 16384
COLS = 32
FEAT = 32
WIDE = 256
CHUNK = 4
PER = MAXB // CHUNK
UNROLL = 8
LIST = TB * PER + UNROLL
MIB = 1024 * 1024

F32 = jnp.float32
BF16 = jnp.bfloat16
NT = (((1,), (1,)), ((), ()))


def dot(left, right):
    return jnp.dot(left, right, preferred_element_type=F32)


def dot_nt(left, right):
    return lax.dot_general(left, right, NT, preferred_element_type=F32)


def one_hot_rows(low_row):
    n = low_row.shape[1]
    rows = lax.broadcasted_iota(jnp.int32, (WIDE, n), 0)
    return jnp.where(rows == low_row, 1.0, 0.0).astype(BF16)


def list_chunks(cnt_ref, tiles_ref, buf_ref, sem_ref, list_ref):
    def fetch(chunk):
        span = pl.ds(chunk * CHUNK, CHUNK)
        return pltpu.make_async_copy(tiles_ref.at[span], buf_ref.at[span], sem_ref.at[chunk])

    def block(b, total):
        chunks = (cnt_ref[b] + (CHUNK - 1)) // CHUNK
        for k in range(PER):
            list_ref[total + k] = b * PER + k

            @pl.when(k < chunks)
            def _():
                fetch(b * PER + k).start()

        return total + chunks

    total = lax.fori_loop(0, TB, block, jnp.int32(0))
    for u in range(UNROLL):
        list_ref[total + u] = 0

    def wait():
        def body(i, carry):
            fetch(list_ref[i]).wait()
            return carry

        lax.fori_loop(0, total, body, 0)

    return total, wait


def chunk_slots(bid_ref, cnt_ref, list_ref, item, total):
    chunk = list_ref[item]
    block = chunk // PER
    first = (chunk % PER) * CHUNK
    count = jnp.where(item < total, cnt_ref[block], 0)
    slots = [(bid_ref[chunk * CHUNK + j], first + j < count) for j in range(CHUNK)]
    return chunk, block, slots


def forward_kernel(
    bid_ref, cnt_ref, feat_ref, tgt_ref, slot_ref, tiles_ref,
    out_ref, tgtq_ref,
    buf_ref, sem_ref, list_ref, place_ref, agg_ref,
):
    total, wait = list_chunks(cnt_ref, tiles_ref, buf_ref, sem_ref, list_ref)

    slot = slot_ref[...]
    slot_hi = (slot // WIDE).astype(F32)
    slot_lo = slot % WIDE
    for i in range(TGT // WIDE):
        span = slice(i * WIDE, (i + 1) * WIDE)
        place_ref[:, span] = one_hot_rows(slot_lo[:, span])

    tgt = tgt_ref[...]
    row16 = lax.broadcasted_iota(jnp.int32, (16, TGT), 0)
    parts = jnp.where(row16 == 0, tgt // WIDE, jnp.where(row16 == 1, tgt % WIDE, 0)).astype(BF16)
    hi16 = jnp.broadcast_to(slot_hi, (16, TGT)).astype(BF16)

    def masked(values, wanted):
        reps = values.shape[0] // 16
        mask = hi16 == jnp.asarray(wanted, BF16)
        pieces = [
            jnp.where(mask, values[r * 16:(r + 1) * 16], jnp.zeros((), BF16)) for r in range(reps)
        ]
        return pieces

    rows = []
    for q in range(TGT // WIDE):
        rows += masked(parts, q)
    moved = dot_nt(jnp.concatenate(rows, axis=0), place_ref[...])
    for q in range(TGT // WIDE):
        tgtq_ref[:, q * WIDE:(q + 1) * WIDE] = moved[q * 16:q * 16 + 8]

    group = 32

    def gather(i, carry):
        span = pl.ds(pl.multiple_of(i * WIDE, WIDE), WIDE)
        ids = tgtq_ref[:, span]
        high = jnp.broadcast_to(ids[0:1], (8, WIDE))
        marks = one_hot_rows(ids[1:2].astype(jnp.int32))
        acc = [jnp.zeros((8, WIDE), F32) for _ in range(COLS // 8)]
        for g in range(NODES // WIDE // group):
            left = jnp.concatenate(
                [
                    feat_ref[:, (g * group + n) * WIDE:(g * group + n + 1) * WIDE]
                    for n in range(group)
                ],
                axis=0,
            )
            prod = dot(left, marks)
            for n in range(group):
                mask = high == float(g * group + n)
                for c in range(COLS // 8):
                    at = n * COLS + c * 8
                    acc[c] = jnp.where(mask, prod[at:at + 8], acc[c])
        own = jnp.concatenate(acc, axis=0).astype(BF16)
        out_ref[2 * i, 0:COLS] = own[:, :BLK]
        out_ref[2 * i + 1, 0:COLS] = own[:, BLK:]
        return carry

    lax.fori_loop(0, TGT // WIDE, gather, 0)

    agg_ref[...] = jnp.zeros_like(agg_ref)
    wait()

    def aggregate(i, carry):
        done = []
        for u in range(UNROLL):
            chunk, block, slots = chunk_slots(bid_ref, cnt_ref, list_ref, i * UNROLL + u, total)
            left = []
            for node_block, live in slots:
                span = pl.ds(pl.multiple_of(node_block * BLK, BLK), BLK)
                left.append(jnp.where(live, feat_ref[:, span], jnp.zeros((), BF16)))
            tiles = buf_ref[pl.ds(chunk * CHUNK, CHUNK)].reshape(CHUNK * BLK, BLK)
            done.append((block, dot(jnp.concatenate(left, axis=1), tiles)))
        for block, prod in done:
            span = pl.ds(pl.multiple_of(block * BLK, BLK), BLK)
            agg_ref[:, span] += prod
        return carry

    lax.fori_loop(0, (total + UNROLL - 1) // UNROLL, aggregate, 0)

    aggregate_rows = agg_ref[...].astype(BF16)
    half = 8
    for g in range(TGT // WIDE // half):
        rows = []
        for q in range(half):
            rows += masked(aggregate_rows, g * half + q)
        moved = dot_nt(jnp.concatenate(rows, axis=0), place_ref[...]).astype(BF16)
        for q in range(half):
            piece = moved[q * COLS:(q + 1) * COLS]
            out_ref[2 * (g * half + q), COLS:] = piece[:, :BLK]
            out_ref[2 * (g * half + q) + 1, COLS:] = piece[:, BLK:]


VMEM = pl.BlockSpec(memory_space=pltpu.VMEM)
SMEM = pl.BlockSpec(memory_space=pltpu.SMEM)
HBM = pl.BlockSpec(memory_space=pl.ANY)


def params(mib):
    return pltpu.CompilerParams(vmem_limit_bytes=mib * MIB)


def forward(block_list, counts, features, targets, slots, tiles):
    return pl.pallas_call(
        forward_kernel,
        out_shape=(
            jax.ShapeDtypeStruct((FEAT, 2 * COLS, BLK), BF16),
            jax.ShapeDtypeStruct((8, TGT), F32),
        ),
        in_specs=[SMEM, SMEM, VMEM, VMEM, VMEM, HBM],
        out_specs=(VMEM, VMEM),
        scratch_shapes=[
            pltpu.VMEM((TB * MAXB, BLK, BLK), BF16),
            pltpu.SemaphoreType.DMA((TB * PER,)),
            pltpu.SMEM((LIST,), jnp.int32),
            pltpu.VMEM((WIDE, TGT), BF16),
            pltpu.VMEM((COLS, TGT), F32),
        ],
        compiler_params=params(48),
        name="gather_and_aggregate",
    )(block_list, counts, features, targets, slots, tiles)


def middle_kernel(x_ref, w_ref, bias_ref, grad_ref, hidden_ref, back_ref, wgrad_ref):
    x = x_ref[...].reshape(FEAT * 2 * COLS, BLK)
    w = w_ref[...]
    preact = lax.dot_general(x, w, (((0,), (0,)), ((), ())), preferred_element_type=F32)
    preact = preact + bias_ref[...]
    sig = jax.nn.sigmoid(preact)
    hidden_ref[...] = (preact * sig).astype(BF16)
    slope = (grad_ref[...].astype(F32) * sig * (1.0 + preact * (1.0 - sig))).astype(BF16)
    back_ref[...] = dot_nt(w, slope).astype(BF16).reshape(FEAT, 2 * COLS, BLK)
    wgrad_ref[:, :2 * COLS, :] = dot(x, slope).astype(BF16).reshape(FEAT, 2 * COLS, WIDE)
    total = jnp.sum(slope.astype(F32), axis=0, keepdims=True)
    first = total.astype(BF16)
    rest = total - first.astype(F32)
    second = rest.astype(BF16)
    third = (rest - second.astype(F32)).astype(BF16)
    row = lax.broadcasted_iota(jnp.int32, (16, WIDE), 0)
    tail = jnp.where(
        row == 0,
        first.astype(F32),
        jnp.where(row == 1, second.astype(F32), jnp.where(row == 2, third.astype(F32), 0.0)),
    ).astype(BF16)
    wgrad_ref[:, 2 * COLS:, :] = jnp.broadcast_to(tail[None], (FEAT, 16, WIDE))


def middle(x, w, bias, grad):
    return pl.pallas_call(
        middle_kernel,
        out_shape=(
            jax.ShapeDtypeStruct((BLK, WIDE), BF16),
            jax.ShapeDtypeStruct((FEAT, 2 * COLS, BLK), BF16),
            jax.ShapeDtypeStruct((FEAT, 2 * COLS + 16, WIDE), BF16),
        ),
        in_specs=[VMEM] * 4,
        out_specs=(VMEM,) * 3,
        compiler_params=params(32),
        name="hidden_and_slope",
    )(x, w, bias, grad)


def backward_kernel(
    zid_ref, bid_ref, cnt_ref, back_ref, slot_ref, tgtq_ref, tiles_ref,
    near_ref, far_ref,
    buf_ref, sem_ref, list_ref, rows_ref, grad_ref, mark_ref,
):
    total, wait = list_chunks(cnt_ref, tiles_ref, buf_ref, sem_ref, list_ref)

    slot = slot_ref[...]
    slot_hi = (slot // WIDE).astype(F32)
    slot_lo = slot % WIDE
    pairs = TGT // WIDE

    left = jnp.concatenate(
        [
            jnp.concatenate([back_ref[2 * q, COLS:], back_ref[2 * q + 1, COLS:]], axis=1)
            for q in range(pairs)
        ],
        axis=0,
    )
    for i in range(TGT // WIDE):
        span = slice(i * WIDE, (i + 1) * WIDE)
        prod = dot(left, one_hot_rows(slot_lo[:, span]))
        high = jnp.broadcast_to(slot_hi[:, span], (8, WIDE))
        acc = [jnp.zeros((8, WIDE), F32) for _ in range(COLS // 8)]
        for q in range(pairs):
            mask = high == float(q)
            for c in range(COLS // 8):
                at = q * COLS + c * 8
                acc[c] = jnp.where(mask, prod[at:at + 8], acc[c])
        rows_ref[:, span] = jnp.concatenate(acc, axis=0).astype(BF16)

    grad_ref[...] = jnp.zeros_like(grad_ref)
    wait()

    def spread(i, carry):
        done = []
        for u in range(UNROLL):
            chunk, block, slots = chunk_slots(bid_ref, cnt_ref, list_ref, i * UNROLL + u, total)
            span = pl.ds(pl.multiple_of(block * BLK, BLK), BLK)
            tiles = buf_ref[pl.ds(chunk * CHUNK, CHUNK)].reshape(CHUNK * BLK, BLK)
            done.append((slots, dot_nt(rows_ref[:, span], tiles)))
        for slots, prod in done:
            for j, (node_block, live) in enumerate(slots):
                piece = prod[:, j * BLK:(j + 1) * BLK]
                span = pl.ds(pl.multiple_of(node_block * BLK, BLK), BLK)
                grad_ref[:, span] += jnp.where(live, piece, 0.0)
        return carry

    lax.fori_loop(0, (total + UNROLL - 1) // UNROLL, spread, 0)

    ids = tgtq_ref[...]
    for i in range(TGT // WIDE):
        span = slice(i * WIDE, (i + 1) * WIDE)
        mark_ref[:, span] = one_hot_rows(ids[1:2, span].astype(jnp.int32))
    hi16 = jnp.broadcast_to(ids[0:1], (16, TGT)).astype(BF16)
    own = jnp.concatenate([back_ref[q, :COLS] for q in range(FEAT)], axis=1)
    quarter = NODES // 4
    per = quarter // WIDE
    half = 8

    def scatter(step, carry):
        which = lax.rem(zid_ref[0] + step, 4)
        for g in range(per // half):
            rows = []
            for n in range(half):
                wanted = (which * per + g * half + n).astype(F32).astype(BF16)
                mask = hi16 == wanted
                for r in range(COLS // 16):
                    rows.append(
                        jnp.where(mask, own[r * 16:(r + 1) * 16], jnp.zeros((), BF16))
                    )
            prod = dot_nt(jnp.concatenate(rows, axis=0), mark_ref[...])
            for n in range(half):
                at = (g * half + n) * WIDE
                span = pl.ds(pl.multiple_of(which * quarter + at, WIDE), WIDE)
                value = grad_ref[:, span] + prod[n * COLS:(n + 1) * COLS]

                @pl.when(step == 0)
                def _():
                    near_ref[:, at:at + WIDE] = value

                @pl.when(step > 0)
                def _():
                    far_ref[jnp.maximum(step - 1, 0), :, at:at + WIDE] = value.astype(BF16)

        return carry

    lax.fori_loop(0, 4, scatter, 0)


def backward(zid, block_list, counts, back, slots, tgtq, tiles):
    return pl.pallas_call(
        backward_kernel,
        out_shape=(
            jax.ShapeDtypeStruct((COLS, NODES // 4), F32),
            jax.ShapeDtypeStruct((3, COLS, NODES // 4), BF16),
        ),
        in_specs=[SMEM, SMEM, SMEM, VMEM, VMEM, VMEM, HBM],
        out_specs=(VMEM, VMEM),
        scratch_shapes=[
            pltpu.VMEM((TB * MAXB, BLK, BLK), BF16),
            pltpu.SemaphoreType.DMA((TB * PER,)),
            pltpu.SMEM((LIST,), jnp.int32),
            pltpu.VMEM((COLS, TGT), BF16),
            pltpu.VMEM((COLS, NODES), F32),
            pltpu.VMEM((WIDE, TGT), BF16),
        ],
        compiler_params=params(48),
        name="spread_and_scatter",
    )(zid, block_list, counts, back, slots, tgtq, tiles)


def place_kernel(zid_ref, a_ref, b_ref, c_ref, d_ref, out_ref):
    quarter = NODES // 4
    for step, ref in enumerate((a_ref, b_ref, c_ref, d_ref)):
        at = pl.multiple_of(lax.rem(zid_ref[0] + step, 4) * quarter, quarter)
        out_ref[:, pl.ds(at, quarter)] = ref[...].astype(F32)


def place(zid, quarters):
    return pl.pallas_call(
        place_kernel,
        out_shape=jax.ShapeDtypeStruct((COLS, NODES), F32),
        in_specs=[SMEM] + [VMEM] * 4,
        out_specs=VMEM,
        compiler_params=params(32),
        name="place_quarters",
    )(zid, *quarters)


def shift(value, by):
    return lax.ppermute(value, "dp", [(k, (k + by) % 4) for k in range(4)])


def shards(
    features,
    targets,
    block_ids,
    counts,
    target_slots,
    edge_tiles,
    self_weight,
    neigh_weight,
    hidden_bias,
    hidden_grad,
):
    tiles = edge_tiles.reshape(TB * MAXB, BLK, BLK)
    block_list = block_ids.reshape(-1)
    live = counts.reshape(-1)
    zid = lax.axis_index("dp").astype(jnp.int32).reshape(1)

    weights = lax.all_gather(
        jnp.concatenate([self_weight, neigh_weight], axis=0), "feat", axis=0, tiled=True
    )
    sent, tgtq = forward(block_list, live, features, targets, target_slots, tiles)
    got = lax.all_to_all(sent, "feat", 0, 0, tiled=True)
    hidden, back, wgrad = middle(got, weights, hidden_bias.reshape(1, -1), hidden_grad[0])
    back = lax.all_to_all(back, "feat", 0, 0, tiled=True)
    near, far = backward(zid, block_list, live, back, target_slots, tgtq, tiles)

    wgrad = lax.all_to_all(wgrad, "feat", 0, 0, tiled=True)
    wsum = jnp.sum(wgrad.astype(F32), axis=0)
    wsum = (wsum + shift(wsum, 2)) + (shift(wsum, 1) + shift(wsum, 3))
    self_grad = wsum[:COLS]
    neigh_grad = wsum[COLS:2 * COLS]
    bias_grad = wsum[2 * COLS] + (wsum[2 * COLS + 1] + wsum[2 * COLS + 2])

    one, two, three = shift(far[0], 1), shift(far[1], 2), shift(far[2], 3)
    done = (near + one.astype(F32) + two.astype(F32) + three.astype(F32)).astype(BF16)
    feature_grad = place(zid, (done, shift(done, 3), shift(done, 2), shift(done, 1)))
    return (hidden[None], feature_grad, self_grad, neigh_grad, bias_grad)


def solution(mesh):
    return jax.shard_map(
        shards,
        mesh=mesh,
        in_specs=(
            P("feat", None),
            P("dp", None),
            P("dp", None, None),
            P("dp", None),
            P("dp", None),
            P("dp", None, None, None, None),
            P("feat", None),
            P("feat", None),
            P(),
            P("dp", "feat", None),
        ),
        out_specs=(P("dp", "feat", None), P("feat", None), P("feat", None), P("feat", None), P()),
        check_vma=False,
    )
```

```python
import jax
import jax.numpy as jnp
from jax import lax
from jax.experimental import pallas as pl
from jax.experimental.pallas import tpu as pltpu
from jax.sharding import PartitionSpec as P

BLK = 128
MAXB = 16
TB = 32
NBLK = 128
TGT = 4096
NODES = 16384
COLS = 32
FEAT = 32
WIDE = 256
CHUNK = 4
PER = MAXB // CHUNK
UNROLL = 8
LIST = TB * PER + UNROLL
MIB = 1024 * 1024

F32 = jnp.float32
BF16 = jnp.bfloat16
NT = (((1,), (1,)), ((), ()))


def dot(left, right):
    return jnp.dot(left, right, preferred_element_type=F32)


def dot_nt(left, right):
    return lax.dot_general(left, right, NT, preferred_element_type=F32)


def one_hot_rows(low_row):
    n = low_row.shape[1]
    rows = lax.broadcasted_iota(jnp.int32, (WIDE, n), 0)
    return jnp.where(rows == low_row, 1.0, 0.0).astype(BF16)


def list_chunks(cnt_ref, list_ref, tiles_ref, buf_ref, sem_ref):
    def fetch(chunk):
        span = pl.ds(chunk * CHUNK, CHUNK)
        return pltpu.make_async_copy(tiles_ref.at[span], buf_ref.at[span], sem_ref.at[chunk])

    def block(b, total):
        chunks = (cnt_ref[0, b] + (CHUNK - 1)) // CHUNK
        for k in range(PER):
            list_ref[total + k] = b * PER + k

            @pl.when(k < chunks)
            def _():
                fetch(b * PER + k).start()

        return total + chunks

    total = lax.fori_loop(0, TB, block, jnp.int32(0))
    for u in range(UNROLL):
        list_ref[total + u] = 0

    def wait():
        def body(i, carry):
            fetch(list_ref[i]).wait()
            return carry

        lax.fori_loop(0, total, body, 0)

    return total, wait


def chunk_slots(bid_ref, cnt_ref, list_ref, item, total):
    chunk = list_ref[item]
    block = chunk // PER
    first = (chunk % PER) * CHUNK
    count = jnp.where(item < total, cnt_ref[0, block], 0)
    slots = [(bid_ref[0, block, first + j], first + j < count) for j in range(CHUNK)]
    return chunk, block, slots


def place_marks(slot_ref, place_ref):
    slot = slot_ref[...]
    slot_lo = slot % WIDE
    for i in range(TGT // WIDE):
        span = slice(i * WIDE, (i + 1) * WIDE)
        place_ref[:, span] = one_hot_rows(slot_lo[:, span])
    return jnp.broadcast_to((slot // WIDE).astype(F32), (16, TGT)).astype(BF16)


def keep(values, high, wanted):
    mask = high == jnp.asarray(wanted, BF16)
    return [
        jnp.where(mask, values[r:r + 16], jnp.zeros((), BF16)) for r in range(0, values.shape[0], 16)
    ]


def forward_kernel(
    bid_ref, cnt_ref, feat_ref, tgt_ref, slot_ref, tiles_ref,
    out_ref, tgtq_ref,
    buf_ref, sem_ref, list_ref, place_ref, agg_ref,
):
    total, wait = list_chunks(cnt_ref, list_ref, tiles_ref, buf_ref, sem_ref)
    high16 = place_marks(slot_ref, place_ref)
    tgt = tgt_ref[...]
    row16 = lax.broadcasted_iota(jnp.int32, (16, TGT), 0)
    parts = jnp.where(row16 == 0, tgt // WIDE, jnp.where(row16 == 1, tgt % WIDE, 0)).astype(BF16)
    rows = []
    for q in range(TGT // WIDE):
        rows += keep(parts, high16, q)
    moved = dot_nt(jnp.concatenate(rows, axis=0), place_ref[...])
    for q in range(TGT // WIDE):
        tgtq_ref[:, q * WIDE:(q + 1) * WIDE] = moved[q * 16:q * 16 + 8]

    group = 32

    def gather(i, carry):
        span = pl.ds(pl.multiple_of(i * WIDE, WIDE), WIDE)
        ids = tgtq_ref[:, span]
        high = jnp.broadcast_to(ids[0:1], (8, WIDE))
        marks = one_hot_rows(ids[1:2].astype(jnp.int32))
        acc = [jnp.zeros((8, WIDE), F32) for _ in range(COLS // 8)]
        for g in range(NODES // WIDE // group):
            left = jnp.concatenate(
                [
                    feat_ref[:, (g * group + n) * WIDE:(g * group + n + 1) * WIDE]
                    for n in range(group)
                ],
                axis=0,
            )
            prod = dot(left, marks)
            for n in range(group):
                mask = high == float(g * group + n)
                for c in range(COLS // 8):
                    at = n * COLS + c * 8
                    acc[c] = jnp.where(mask, prod[at:at + 8], acc[c])
        own = jnp.concatenate(acc, axis=0).astype(BF16)
        out_ref[2 * i, :COLS] = own[:, :BLK]
        out_ref[2 * i + 1, :COLS] = own[:, BLK:]
        return carry

    lax.fori_loop(0, TGT // WIDE, gather, 0)

    agg_ref[...] = jnp.zeros_like(agg_ref)
    wait()

    def aggregate(i, carry):
        done = []
        for u in range(UNROLL):
            chunk, block, slots = chunk_slots(bid_ref, cnt_ref, list_ref, i * UNROLL + u, total)
            left = []
            for node_block, live in slots:
                span = pl.ds(pl.multiple_of(node_block * BLK, BLK), BLK)
                left.append(jnp.where(live, feat_ref[:, span], jnp.zeros((), BF16)))
            tiles = buf_ref[pl.ds(chunk * CHUNK, CHUNK)].reshape(CHUNK * BLK, BLK)
            done.append((block, dot(jnp.concatenate(left, axis=1), tiles)))
        for block, prod in done:
            span = pl.ds(pl.multiple_of(block * BLK, BLK), BLK)
            agg_ref[:, span] += prod
        return carry

    lax.fori_loop(0, (total + UNROLL - 1) // UNROLL, aggregate, 0)

    aggregate_rows = agg_ref[...].astype(BF16)
    half = 8
    for g in range(TGT // WIDE // half):
        rows = []
        for q in range(half):
            rows += keep(aggregate_rows, high16, g * half + q)
        moved = dot_nt(jnp.concatenate(rows, axis=0), place_ref[...]).astype(BF16)
        for q in range(half):
            piece = moved[q * COLS:(q + 1) * COLS]
            out_ref[2 * (g * half + q), COLS:] = piece[:, :BLK]
            out_ref[2 * (g * half + q) + 1, COLS:] = piece[:, BLK:]


VMEM = pl.BlockSpec(memory_space=pltpu.VMEM)
SMEM = pl.BlockSpec(memory_space=pltpu.SMEM)


HBM = pl.BlockSpec(memory_space=pl.ANY)


def params(mib):
    return pltpu.CompilerParams(vmem_limit_bytes=mib * MIB)


def cost(microseconds):
    return pl.CostEstimate(
        flops=microseconds * 1100 * MIB,
        bytes_accessed=int(microseconds * 3.5 * MIB),
        transcendentals=0,
    )


BLOCKS = jax.ShapeDtypeStruct((FEAT, 2 * COLS, BLK), BF16)
TILE_BUFFER = [
    pltpu.VMEM((TB * MAXB, BLK, BLK), BF16),
    pltpu.SemaphoreType.DMA((TB * PER,)),
    pltpu.SMEM((LIST,), jnp.int32),
]


def forward(block_ids, counts, features, targets, slots, tiles):
    return pl.pallas_call(
        forward_kernel,
        out_shape=(
            BLOCKS,
            jax.ShapeDtypeStruct((8, TGT), F32),
        ),
        in_specs=[SMEM, SMEM, VMEM, VMEM, VMEM, HBM],
        out_specs=(VMEM, VMEM),
        scratch_shapes=TILE_BUFFER
        + [pltpu.VMEM((WIDE, TGT), BF16), pltpu.VMEM((COLS, TGT), F32)],
        compiler_params=params(40),
        cost_estimate=cost(15),
        name="gather_and_aggregate",
    )(block_ids, counts, features, targets, slots, tiles)


def middle_kernel(
    x_ref, w_ref, bias_ref, grad_ref, hidden_ref, back_ref, wgrad_ref
):
    half = FEAT * COLS
    x_own = x_ref[:, :COLS].reshape(half, BLK)
    x_agg = x_ref[:, COLS:].reshape(half, BLK)
    w_own = w_ref[:, :COLS].reshape(half, WIDE)
    w_agg = w_ref[:, COLS:].reshape(half, WIDE)
    tn = (((0,), (0,)), ((), ()))
    preact = lax.dot_general(x_own, w_own, tn, preferred_element_type=F32)
    preact = preact + lax.dot_general(x_agg, w_agg, tn, preferred_element_type=F32)
    preact = preact + bias_ref[...]
    sig = jax.nn.sigmoid(preact)
    hidden_ref[0] = (preact * sig).astype(BF16)
    slope = (grad_ref[0].astype(F32) * sig * (1.0 + preact * (1.0 - sig))).astype(BF16)
    back_ref[:, :COLS] = dot_nt(w_own, slope).astype(BF16).reshape(FEAT, COLS, BLK)
    back_ref[:, COLS:] = dot_nt(w_agg, slope).astype(BF16).reshape(FEAT, COLS, BLK)
    wgrad_ref[:, :COLS] = dot(x_own, slope).astype(BF16).reshape(FEAT, COLS, WIDE)
    wgrad_ref[:, COLS:2 * COLS] = dot(x_agg, slope).astype(BF16).reshape(FEAT, COLS, WIDE)
    total = jnp.sum(slope.astype(F32), axis=0, keepdims=True)
    first = total.astype(BF16).astype(F32)
    rest = total - first
    second = rest.astype(BF16).astype(F32)
    third = rest - second
    row = lax.broadcasted_iota(jnp.int32, (16, WIDE), 0)
    tail = jnp.where(
        row == 0, first, jnp.where(row == 1, second, jnp.where(row == 2, third, 0.0))
    ).astype(BF16)
    wgrad_ref[:, 2 * COLS:] = jnp.broadcast_to(tail[None], (FEAT, 16, WIDE))


def middle(x, w, bias, grad):
    return pl.pallas_call(
        middle_kernel,
        out_shape=(
            jax.ShapeDtypeStruct((1, BLK, WIDE), BF16),
            BLOCKS,
            jax.ShapeDtypeStruct((FEAT, 2 * COLS + 16, WIDE), BF16),
        ),
        in_specs=[VMEM] * 4,
        out_specs=(VMEM,) * 3,
        compiler_params=params(24),
        cost_estimate=cost(2),
        name="hidden_and_slope",
    )(x, w, bias, grad)


def spread_kernel(
    bid_ref, cnt_ref, back_ref, slot_ref, tiles_ref, grad_ref, buf_ref, sem_ref, list_ref, rows_ref
):
    total, wait = list_chunks(cnt_ref, list_ref, tiles_ref, buf_ref, sem_ref)
    slot = slot_ref[...]
    slot_hi = (slot // WIDE).astype(F32)
    slot_lo = slot % WIDE
    pairs = TGT // WIDE
    left = jnp.concatenate(
        [jnp.concatenate([back_ref[2 * q, COLS:], back_ref[2 * q + 1, COLS:]], axis=1) for q in range(pairs)],
        axis=0,
    )
    for i in range(TGT // WIDE):
        span = slice(i * WIDE, (i + 1) * WIDE)
        prod = dot(left, one_hot_rows(slot_lo[:, span]))
        high = jnp.broadcast_to(slot_hi[:, span], (8, WIDE))
        acc = [jnp.zeros((8, WIDE), F32) for _ in range(COLS // 8)]
        for q in range(pairs):
            mask = high == float(q)
            for c in range(COLS // 8):
                at = q * COLS + c * 8
                acc[c] = jnp.where(mask, prod[at:at + 8], acc[c])
        rows_ref[:, span] = jnp.concatenate(acc, axis=0).astype(BF16)

    grad_ref[...] = jnp.zeros_like(grad_ref)
    wait()

    def spread(i, carry):
        done = []
        for u in range(UNROLL):
            chunk, block, slots = chunk_slots(bid_ref, cnt_ref, list_ref, i * UNROLL + u, total)
            span = pl.ds(pl.multiple_of(block * BLK, BLK), BLK)
            tiles = buf_ref[pl.ds(chunk * CHUNK, CHUNK)].reshape(CHUNK * BLK, BLK)
            done.append((slots, dot_nt(rows_ref[:, span], tiles)))
        for slots, prod in done:
            for j, (node_block, live) in enumerate(slots):
                piece = prod[:, j * BLK:(j + 1) * BLK]
                span = pl.ds(pl.multiple_of(node_block * BLK, BLK), BLK)
                grad_ref[:, span] += jnp.where(live, piece, 0.0)
        return carry

    lax.fori_loop(0, (total + UNROLL - 1) // UNROLL, spread, 0)


def spread_part(block_ids, counts, back, slots, tiles):
    return pl.pallas_call(
        spread_kernel,
        out_shape=jax.ShapeDtypeStruct((COLS, NODES), F32),
        in_specs=[SMEM, SMEM, VMEM, VMEM, HBM],
        out_specs=VMEM,
        scratch_shapes=TILE_BUFFER + [pltpu.VMEM((COLS, TGT), BF16)],
        compiler_params=params(40),
        cost_estimate=cost(7),
        name="spread",
    )(block_ids, counts, back, slots, tiles)


QUARTER = NODES // 4


def scatter_kernel(zid_ref, grad_ref, back_ref, tgtq_ref, *refs, steps):
    out_refs, mark_ref = refs[:-1], refs[-1]
    ids = tgtq_ref[...]
    for i in range(TGT // WIDE):
        span = slice(i * WIDE, (i + 1) * WIDE)
        mark_ref[:, span] = one_hot_rows(ids[1:2, span].astype(jnp.int32))
    high16 = jnp.broadcast_to(ids[0:1], (16, TGT)).astype(BF16)
    own = jnp.concatenate([back_ref[q, :COLS] for q in range(FEAT)], axis=1)
    per = QUARTER // WIDE
    half = 8
    for step, out_ref in zip(steps, out_refs):
        which = lax.rem(zid_ref[0] + step, 4)
        for g in range(per // half):
            rows = []
            for n in range(half):
                wanted = (which * per + g * half + n).astype(F32).astype(BF16)
                rows += keep(own, high16, wanted)
            prod = dot_nt(jnp.concatenate(rows, axis=0), mark_ref[...])
            for n in range(half):
                at = (g * half + n) * WIDE
                span = pl.ds(pl.multiple_of(which * QUARTER + at, WIDE), WIDE)
                value = grad_ref[:, span] + prod[n * COLS:(n + 1) * COLS]
                out_ref[:, at:at + WIDE] = value.astype(out_ref.dtype)


def scatter_part(zid, grad, back, tgtq, steps):
    return pl.pallas_call(
        lambda *refs: scatter_kernel(*refs, steps=steps),
        out_shape=tuple(
            jax.ShapeDtypeStruct((COLS, QUARTER), BF16 if step else F32) for step in steps
        ),
        in_specs=[SMEM, VMEM, VMEM, VMEM],
        out_specs=tuple(VMEM for _ in steps),
        scratch_shapes=[pltpu.VMEM((WIDE, TGT), BF16)],
        compiler_params=params(24),
        cost_estimate=cost(1 + len(steps)),
        name="scatter",
    )(zid, grad, back, tgtq)


def place_kernel(zid_ref, a_ref, b_ref, c_ref, d_ref, out_ref):
    quarter = NODES // 4
    for step, ref in enumerate((a_ref, b_ref, c_ref, d_ref)):
        at = pl.multiple_of(lax.rem(zid_ref[0] + step, 4) * quarter, quarter)
        out_ref[:, pl.ds(at, quarter)] = ref[...].astype(F32)


def place(zid, quarters):
    return pl.pallas_call(
        place_kernel,
        out_shape=jax.ShapeDtypeStruct((COLS, NODES), F32),
        in_specs=[SMEM] + [VMEM] * 4,
        out_specs=VMEM,
        compiler_params=params(32),
        cost_estimate=cost(1),
        name="place_quarters",
    )(zid, *quarters)


def shift(value, by):
    return lax.ppermute(value, "dp", [(k, (k + by) % 4) for k in range(4)])


def relay(value):
    pairs = [
        (k * FEAT + f, ((k + (1 if f % 2 == 0 else 3)) % 4) * FEAT + f)
        for k in range(4)
        for f in range(FEAT)
    ]
    return lax.ppermute(value, ("dp", "feat"), pairs)


def exchange(value):
    return lax.all_to_all(value, "feat", 0, 0, tiled=True)


def shards(
    features,
    targets,
    block_ids,
    counts,
    target_slots,
    edge_tiles,
    self_weight,
    neigh_weight,
    hidden_bias,
    hidden_grad,
):
    tiles = edge_tiles.reshape(TB * MAXB, BLK, BLK)
    zid = lax.axis_index("dp").astype(jnp.int32).reshape(1)

    side = lax.axis_index("feat") % 2

    weights = jnp.concatenate([self_weight, neigh_weight], axis=0)
    weights = exchange(jnp.broadcast_to(weights[None], (FEAT, 2 * COLS, WIDE)))
    sent, tgtq = forward(block_ids, counts, features, targets, target_slots, tiles)
    sent, weights = lax.optimization_barrier((sent, weights))
    hidden, back, wgrad = middle(
        exchange(sent), weights, hidden_bias.reshape(1, -1), hidden_grad
    )
    back = exchange(back)
    grad = spread_part(block_ids, counts, back, target_slots, tiles)
    (far2,) = scatter_part(zid, grad, back, tgtq, (2,))
    grad, far2 = lax.optimization_barrier((grad, far2))
    far1, far3 = scatter_part(zid, grad, back, tgtq, (1, 3))
    grad, far1, far3, wgrad = lax.optimization_barrier((grad, far1, far3, wgrad))
    (near,) = scatter_part(zid, grad, back, tgtq, (0,))

    relayed = relay(far2)
    to_next = far1.astype(F32) + jnp.where(side == 0, relayed, 0).astype(F32)
    to_last = far3.astype(F32) + jnp.where(side == 1, relayed, 0).astype(F32)
    from_last, from_next = shift(to_next.astype(BF16), 1), shift(to_last.astype(BF16), 3)

    wgrad = exchange(wgrad)
    wsum = jnp.sum(wgrad.astype(F32), axis=0)
    wsum = (wsum + shift(wsum, 2)) + (shift(wsum, 1) + shift(wsum, 3))
    self_grad = wsum[:COLS]
    neigh_grad = wsum[COLS:2 * COLS]
    bias_grad = wsum[2 * COLS] + (wsum[2 * COLS + 1] + wsum[2 * COLS + 2])

    done = (near + from_last.astype(F32) + from_next.astype(F32)).astype(BF16)
    of_last, of_next = shift(done, 1), shift(done, 3)
    of_far = relay(jnp.where(side == 0, of_last, of_next))
    feature_grad = place(zid, (done, of_next, of_far, of_last))
    return (hidden, feature_grad, self_grad, neigh_grad, bias_grad)


def solution(mesh):
    return jax.shard_map(
        shards,
        mesh=mesh,
        in_specs=(
            P("feat", None),
            P("dp", None),
            P("dp", None, None),
            P("dp", None),
            P("dp", None),
            P("dp", None, None, None, None),
            P("feat", None),
            P("feat", None),
            P(),
            P("dp", "feat", None),
        ),
        out_specs=(P("dp", "feat", None), P("feat", None), P("feat", None), P("feat", None), P()),
        check_vma=False,
    )
```

```python
import jax
import jax.numpy as jnp
from jax import lax
from jax.experimental import pallas as pl
from jax.experimental.pallas import tpu as pltpu
from jax.sharding import PartitionSpec as P

BLK = 128
MAXB = 16
TB = 32
NBLK = 128
TGT = 4096
NODES = 16384
COLS = 32
FEAT = 32
WIDE = 256
CHUNK = 4
PER = MAXB // CHUNK
UNROLL = 16
LOW = 512
GROUP = 32
LIST = TB * PER + UNROLL
MIB = 1024 * 1024

F32 = jnp.float32
BF16 = jnp.bfloat16
NT = (((1,), (1,)), ((), ()))


def dot(left, right):
    return jnp.dot(left, right, preferred_element_type=F32)


def dot_nt(left, right):
    return lax.dot_general(left, right, NT, preferred_element_type=F32)


def one_hot_rows(low_row, count=WIDE):
    n = low_row.shape[1]
    rows = lax.broadcasted_iota(jnp.int32, (count, n), 0)
    return jnp.where(rows == low_row, 1.0, 0.0).astype(BF16)


def list_chunks(cnt_ref, list_ref, tiles_ref, buf_ref, sem_ref):
    def fetch(chunk):
        span = pl.ds(chunk * CHUNK, CHUNK)
        return pltpu.make_async_copy(tiles_ref.at[span], buf_ref.at[span], sem_ref.at[chunk])

    def block(b, total):
        chunks = (cnt_ref[0, b] + (CHUNK - 1)) >> 2
        for k in range(PER):
            list_ref[total + k] = b * PER + k

            @pl.when(k < chunks)
            def _():
                fetch(b * PER + k).start()

        return total + chunks

    total = lax.fori_loop(0, TB, block, jnp.int32(0))
    for u in range(UNROLL):
        list_ref[total + u] = 0

    def wait(step):
        def body(i, carry):
            fetch(list_ref[i]).wait()
            return carry

        first = step * UNROLL
        lax.fori_loop(first, jnp.minimum(first + UNROLL, total), body, 0)

    return total, wait


def chunk_slots(bid_ref, cnt_ref, list_ref, item, total):
    chunk = list_ref[item]
    block = chunk >> 2
    first = (chunk & (PER - 1)) * CHUNK
    count = jnp.where(item < total, cnt_ref[0, block], 0)
    slots = [(bid_ref[0, block, first + j], first + j < count) for j in range(CHUNK)]
    return chunk, block, slots


def place_marks(slot_ref, place_ref):
    slot = slot_ref[...]
    slot_lo = slot % WIDE
    for i in range(TGT // WIDE):
        span = slice(i * WIDE, (i + 1) * WIDE)
        place_ref[:, span] = one_hot_rows(slot_lo[:, span])
    return jnp.broadcast_to((slot // WIDE).astype(F32), (16, TGT)).astype(BF16)


def keep(values, high, wanted):
    mask = high == jnp.asarray(wanted, BF16)
    return [
        jnp.where(mask, values[r:r + 16], jnp.zeros((), BF16)) for r in range(0, values.shape[0], 16)
    ]


def forward_kernel(
    bid_ref, cnt_ref, feat_ref, tgt_ref, slot_ref, tiles_ref,
    out_ref, tgtq_ref,
    buf_ref, sem_ref, list_ref, place_ref, agg_ref,
):
    total, wait = list_chunks(cnt_ref, list_ref, tiles_ref, buf_ref, sem_ref)
    high16 = place_marks(slot_ref, place_ref)
    tgt = tgt_ref[...]
    row16 = lax.broadcasted_iota(jnp.int32, (16, TGT), 0)
    parts = jnp.where(row16 == 0, tgt // WIDE, jnp.where(row16 == 1, tgt % WIDE, 0)).astype(BF16)
    rows = []
    for q in range(TGT // WIDE):
        rows += keep(parts, high16, q)
    moved = dot_nt(jnp.concatenate(rows, axis=0), place_ref[...])
    for q in range(TGT // WIDE):
        tgtq_ref[:, q * WIDE:(q + 1) * WIDE] = moved[q * 16:q * 16 + 8]

    group = GROUP

    def gather(i, carry):
        span = pl.ds(pl.multiple_of(i * WIDE, WIDE), WIDE)
        ids = tgtq_ref[:, span]
        whole = (ids[0:1] * float(WIDE) + ids[1:2]).astype(jnp.int32)
        high = jnp.broadcast_to((whole // LOW).astype(F32), (8, WIDE))
        marks = one_hot_rows(whole % LOW, LOW)
        acc = [jnp.zeros((8, WIDE), F32) for _ in range(COLS // 8)]
        for g in range(NODES // LOW // group):
            left = jnp.concatenate(
                [
                    feat_ref[:, (g * group + n) * LOW:(g * group + n + 1) * LOW]
                    for n in range(group)
                ],
                axis=0,
            )
            prod = dot(left, marks)
            for n in range(group):
                mask = high == float(g * group + n)
                for c in range(COLS // 8):
                    at = n * COLS + c * 8
                    acc[c] = jnp.where(mask, prod[at:at + 8], acc[c])
        own = jnp.concatenate(acc, axis=0).astype(BF16)
        out_ref[2 * i, :COLS] = own[:, :BLK]
        out_ref[2 * i + 1, :COLS] = own[:, BLK:]
        return carry

    lax.fori_loop(0, TGT // WIDE, gather, 0, unroll=2)

    agg_ref[...] = jnp.zeros_like(agg_ref)

    def aggregate(i, carry):
        wait(i)
        done = []
        for u in range(UNROLL):
            chunk, block, slots = chunk_slots(bid_ref, cnt_ref, list_ref, i * UNROLL + u, total)
            left = []
            for node_block, live in slots:
                span = pl.ds(pl.multiple_of(node_block * BLK, BLK), BLK)
                left.append(jnp.where(live, feat_ref[:, span], jnp.zeros((), BF16)))
            tiles = buf_ref[pl.ds(chunk * CHUNK, CHUNK)].reshape(CHUNK * BLK, BLK)
            done.append((block, dot(jnp.concatenate(left, axis=1), tiles)))
        for block, prod in done:
            span = pl.ds(pl.multiple_of(block * BLK, BLK), BLK)
            agg_ref[:, span] += prod
        return carry

    lax.fori_loop(0, (total + UNROLL - 1) >> 4, aggregate, 0)

    aggregate_rows = agg_ref[...].astype(BF16)
    half = 8
    for g in range(TGT // WIDE // half):
        rows = []
        for q in range(half):
            rows += keep(aggregate_rows, high16, g * half + q)
        moved = dot_nt(jnp.concatenate(rows, axis=0), place_ref[...]).astype(BF16)
        for q in range(half):
            piece = moved[q * COLS:(q + 1) * COLS]
            out_ref[2 * (g * half + q), COLS:] = piece[:, :BLK]
            out_ref[2 * (g * half + q) + 1, COLS:] = piece[:, BLK:]


VMEM = pl.BlockSpec(memory_space=pltpu.VMEM)
SMEM = pl.BlockSpec(memory_space=pltpu.SMEM)


HBM = pl.BlockSpec(memory_space=pl.ANY)


def params(mib):
    return pltpu.CompilerParams(vmem_limit_bytes=mib * MIB)


def cost(microseconds):
    return pl.CostEstimate(
        flops=microseconds * 1100 * MIB,
        bytes_accessed=int(microseconds * 3.5 * MIB),
        transcendentals=0,
    )


BLOCKS = jax.ShapeDtypeStruct((FEAT, 2 * COLS, BLK), BF16)
TILE_BUFFER = [
    pltpu.VMEM((TB * MAXB, BLK, BLK), BF16),
    pltpu.SemaphoreType.DMA((TB * PER,)),
    pltpu.SMEM((LIST,), jnp.int32),
]


def forward(block_ids, counts, features, targets, slots, tiles):
    return pl.pallas_call(
        forward_kernel,
        out_shape=(
            BLOCKS,
            jax.ShapeDtypeStruct((8, TGT), F32),
        ),
        in_specs=[SMEM, SMEM, VMEM, VMEM, VMEM, HBM],
        out_specs=(VMEM, VMEM),
        scratch_shapes=TILE_BUFFER
        + [pltpu.VMEM((WIDE, TGT), BF16), pltpu.VMEM((COLS, TGT), F32)],
        compiler_params=params(40),
        cost_estimate=cost(15),
        name="gather_and_aggregate",
    )(block_ids, counts, features, targets, slots, tiles)


def middle_kernel(
    x_ref, w_ref, bias_ref, grad_ref, hidden_ref, back_ref, wgrad_ref
):
    half = FEAT * COLS
    x_own = x_ref[:, :COLS].reshape(half, BLK)
    x_agg = x_ref[:, COLS:].reshape(half, BLK)
    w_own = w_ref[:, :COLS].reshape(half, WIDE)
    w_agg = w_ref[:, COLS:].reshape(half, WIDE)
    tn = (((0,), (0,)), ((), ()))
    preact = lax.dot_general(x_own, w_own, tn, preferred_element_type=F32)
    preact = preact + lax.dot_general(x_agg, w_agg, tn, preferred_element_type=F32)
    preact = preact + bias_ref[...]
    sig = jax.nn.sigmoid(preact)
    hidden_ref[0] = (preact * sig).astype(BF16)
    slope = (grad_ref[0].astype(F32) * sig * (1.0 + preact * (1.0 - sig))).astype(BF16)
    back_ref[:, :COLS] = dot_nt(w_own, slope).astype(BF16).reshape(FEAT, COLS, BLK)
    back_ref[:, COLS:] = dot_nt(w_agg, slope).astype(BF16).reshape(FEAT, COLS, BLK)
    wgrad_ref[:, :COLS] = dot(x_own, slope).astype(BF16).reshape(FEAT, COLS, WIDE)
    wgrad_ref[:, COLS:2 * COLS] = dot(x_agg, slope).astype(BF16).reshape(FEAT, COLS, WIDE)
    total = jnp.sum(slope.astype(F32), axis=0, keepdims=True)
    first = total.astype(BF16).astype(F32)
    rest = total - first
    second = rest.astype(BF16).astype(F32)
    third = rest - second
    row = lax.broadcasted_iota(jnp.int32, (16, WIDE), 0)
    tail = jnp.where(
        row == 0, first, jnp.where(row == 1, second, jnp.where(row == 2, third, 0.0))
    ).astype(BF16)
    wgrad_ref[:, 2 * COLS:] = jnp.broadcast_to(tail[None], (FEAT, 16, WIDE))


def middle(x, w, bias, grad):
    return pl.pallas_call(
        middle_kernel,
        out_shape=(
            jax.ShapeDtypeStruct((1, BLK, WIDE), BF16),
            BLOCKS,
            jax.ShapeDtypeStruct((FEAT, 2 * COLS + 16, WIDE), BF16),
        ),
        in_specs=[VMEM] * 4,
        out_specs=(VMEM,) * 3,
        compiler_params=params(24),
        cost_estimate=cost(2),
        name="hidden_and_slope",
    )(x, w, bias, grad)


def spread_kernel(
    bid_ref, cnt_ref, back_ref, slot_ref, tiles_ref, grad_ref, buf_ref, sem_ref, list_ref, rows_ref
):
    total, wait = list_chunks(cnt_ref, list_ref, tiles_ref, buf_ref, sem_ref)
    slot = slot_ref[...]
    slot_hi = (slot // WIDE).astype(F32)
    slot_lo = slot % WIDE
    pairs = TGT // WIDE
    left = jnp.concatenate(
        [jnp.concatenate([back_ref[2 * q, COLS:], back_ref[2 * q + 1, COLS:]], axis=1) for q in range(pairs)],
        axis=0,
    )
    for i in range(TGT // WIDE):
        span = slice(i * WIDE, (i + 1) * WIDE)
        prod = dot(left, one_hot_rows(slot_lo[:, span]))
        high = jnp.broadcast_to(slot_hi[:, span], (8, WIDE))
        acc = [jnp.zeros((8, WIDE), F32) for _ in range(COLS // 8)]
        for q in range(pairs):
            mask = high == float(q)
            for c in range(COLS // 8):
                at = q * COLS + c * 8
                acc[c] = jnp.where(mask, prod[at:at + 8], acc[c])
        rows_ref[:, span] = jnp.concatenate(acc, axis=0).astype(BF16)

    grad_ref[...] = jnp.zeros_like(grad_ref)

    def spread(i, carry):
        wait(i)
        done = []
        for u in range(UNROLL):
            chunk, block, slots = chunk_slots(bid_ref, cnt_ref, list_ref, i * UNROLL + u, total)
            span = pl.ds(pl.multiple_of(block * BLK, BLK), BLK)
            tiles = buf_ref[pl.ds(chunk * CHUNK, CHUNK)].reshape(CHUNK * BLK, BLK)
            done.append((slots, dot_nt(rows_ref[:, span], tiles)))
        for slots, prod in done:
            for j, (node_block, live) in enumerate(slots):
                piece = prod[:, j * BLK:(j + 1) * BLK]
                span = pl.ds(pl.multiple_of(node_block * BLK, BLK), BLK)
                grad_ref[:, span] += jnp.where(live, piece, 0.0)
        return carry

    lax.fori_loop(0, (total + UNROLL - 1) >> 4, spread, 0)


def spread_part(block_ids, counts, back, slots, tiles):
    return pl.pallas_call(
        spread_kernel,
        out_shape=jax.ShapeDtypeStruct((COLS, NODES), F32),
        in_specs=[SMEM, SMEM, VMEM, VMEM, HBM],
        out_specs=VMEM,
        scratch_shapes=TILE_BUFFER + [pltpu.VMEM((COLS, TGT), BF16)],
        compiler_params=params(40),
        cost_estimate=cost(7),
        name="spread",
    )(block_ids, counts, back, slots, tiles)


QUARTER = NODES // 4


def scatter_kernel(zid_ref, grad_ref, back_ref, tgtq_ref, *refs, steps):
    out_refs, mark_ref = refs[:-1], refs[-1]
    ids = tgtq_ref[...]
    for i in range(TGT // WIDE):
        span = slice(i * WIDE, (i + 1) * WIDE)
        mark_ref[:, span] = one_hot_rows(ids[1:2, span].astype(jnp.int32))
    high16 = jnp.broadcast_to(ids[0:1], (16, TGT)).astype(BF16)
    own = jnp.concatenate([back_ref[q, :COLS] for q in range(FEAT)], axis=1)
    per = QUARTER // WIDE
    half = 8
    for step, out_ref in zip(steps, out_refs):
        which = (zid_ref[0] + step) & 3
        for g in range(per // half):
            rows = []
            for n in range(half):
                wanted = (which * per + g * half + n).astype(F32).astype(BF16)
                rows += keep(own, high16, wanted)
            prod = dot_nt(jnp.concatenate(rows, axis=0), mark_ref[...])
            for n in range(half):
                at = (g * half + n) * WIDE
                span = pl.ds(pl.multiple_of(which * QUARTER + at, WIDE), WIDE)
                value = grad_ref[:, span] + prod[n * COLS:(n + 1) * COLS]
                out_ref[:, at:at + WIDE] = value.astype(out_ref.dtype)


def scatter_part(zid, grad, back, tgtq, steps):
    return pl.pallas_call(
        lambda *refs: scatter_kernel(*refs, steps=steps),
        out_shape=tuple(
            jax.ShapeDtypeStruct((COLS, QUARTER), BF16 if step else F32) for step in steps
        ),
        in_specs=[SMEM, VMEM, VMEM, VMEM],
        out_specs=tuple(VMEM for _ in steps),
        scratch_shapes=[pltpu.VMEM((WIDE, TGT), BF16)],
        compiler_params=params(24),
        cost_estimate=cost(1 + len(steps)),
        name="scatter",
    )(zid, grad, back, tgtq)


def place_kernel(zid_ref, *refs, steps, fresh):
    parts = refs[:len(steps)]
    out_ref, wide_ref, sem = refs[len(steps) + (0 if fresh else 1):]
    copies = []
    for k, (step, ref) in enumerate(zip(steps, parts)):
        at = pl.multiple_of(((zid_ref[0] + step) & 3) * QUARTER, QUARTER)
        wide_ref[k] = ref[...].astype(F32)
        copies.append(
            pltpu.make_async_copy(wide_ref.at[k], out_ref.at[:, pl.ds(at, QUARTER)], sem.at[k])
        )
        copies[-1].start()
    for copy in copies:
        copy.wait()


def place(zid, parts, steps, whole=None):
    count, fresh = len(steps), whole is None
    return pl.pallas_call(
        lambda *refs: place_kernel(*refs, steps=steps, fresh=fresh),
        out_shape=jax.ShapeDtypeStruct((COLS, NODES), F32),
        in_specs=[SMEM] + [VMEM] * count + ([] if fresh else [HBM]),
        out_specs=HBM,
        scratch_shapes=[
            pltpu.VMEM((count, COLS, QUARTER), F32),
            pltpu.SemaphoreType.DMA((count,)),
        ],
        input_output_aliases={} if fresh else {1 + count: 0},
        compiler_params=params(24),
        cost_estimate=cost(1),
        name="place_quarters",
    )(zid, *parts, *(() if fresh else (whole,)))


def shift(value, by):
    return lax.ppermute(value, "dp", [(k, (k + by) % 4) for k in range(4)])


def relay(value):
    pairs = [
        (k * FEAT + f, ((k + (1 if f % 2 == 0 else 3)) % 4) * FEAT + f)
        for k in range(4)
        for f in range(FEAT)
    ]
    return lax.ppermute(value, ("dp", "feat"), pairs)


def exchange(value):
    return lax.all_to_all(value, "feat", 0, 0, tiled=True)


def shards(
    features,
    targets,
    block_ids,
    counts,
    target_slots,
    edge_tiles,
    self_weight,
    neigh_weight,
    hidden_bias,
    hidden_grad,
):
    tiles = edge_tiles.reshape(TB * MAXB, BLK, BLK)
    zid = lax.axis_index("dp").astype(jnp.int32).reshape(1)

    side = lax.axis_index("feat") % 2

    weights = jnp.concatenate([self_weight, neigh_weight], axis=0)
    weights = exchange(jnp.broadcast_to(weights[None], (FEAT, 2 * COLS, WIDE)))
    sent, tgtq = forward(block_ids, counts, features, targets, target_slots, tiles)
    sent, weights = lax.optimization_barrier((sent, weights))
    hidden, back, wgrad = middle(
        exchange(sent), weights, hidden_bias.reshape(1, -1), hidden_grad
    )
    back = exchange(back)
    back, wgrad = lax.optimization_barrier((back, wgrad))
    wgrad = exchange(wgrad)
    grad = spread_part(block_ids, counts, back, target_slots, tiles)
    (far2,) = scatter_part(zid, grad, back, tgtq, (2,))
    grad, far2 = lax.optimization_barrier((grad, far2))
    hop = relay(far2)
    far1, far3, near = scatter_part(zid, grad, back, tgtq, (1, 3, 0))
    from_last, from_next = shift(far1, 1), shift(far3, 3)
    from_far = relay(hop)
    near, wgrad = lax.optimization_barrier((near, wgrad))

    wsum = jnp.sum(wgrad.astype(F32), axis=0)
    wsum = (wsum + shift(wsum, 2)) + (shift(wsum, 1) + shift(wsum, 3))
    self_grad = wsum[:COLS]
    neigh_grad = wsum[COLS:2 * COLS]
    bias_grad = wsum[2 * COLS] + (wsum[2 * COLS + 1] + wsum[2 * COLS + 2])

    done = near + from_last.astype(F32) + from_next.astype(F32) + from_far.astype(F32)
    done = done.astype(BF16)
    of_far, of_next, of_last = shift(done, 2), shift(done, 3), shift(done, 1)
    feature_grad = place(zid, (done,), (0,))
    feature_grad = place(zid, (of_next, of_far, of_last), (1, 2, 3), feature_grad)
    return (hidden, feature_grad, self_grad, neigh_grad, bias_grad)


def solution(mesh):
    return jax.shard_map(
        shards,
        mesh=mesh,
        in_specs=(
            P("feat", None),
            P("dp", None),
            P("dp", None, None),
            P("dp", None),
            P("dp", None),
            P("dp", None, None, None, None),
            P("feat", None),
            P("feat", None),
            P(),
            P("dp", "feat", None),
        ),
        out_specs=(P("dp", "feat", None), P("feat", None), P("feat", None), P("feat", None), P()),
        check_vma=False,
    )
```

```python
import jax
import jax.numpy as jnp
from jax import lax
from jax.experimental import pallas as pl
from jax.experimental.pallas import tpu as pltpu
from jax.sharding import PartitionSpec as P

BLK = 128
MAXB = 16
TB = 32
NBLK = 128
TGT = 4096
NODES = 16384
COLS = 32
FEAT = 32
WIDE = 256
CHUNK = 4
PER = MAXB // CHUNK
UNROLL = 16
LOW = 512
GROUP = 32
LIST = TB * PER + UNROLL
MIB = 1024 * 1024

F32 = jnp.float32
BF16 = jnp.bfloat16
NT = (((1,), (1,)), ((), ()))


def dot(left, right):
    return jnp.dot(left, right, preferred_element_type=F32)


def dot_nt(left, right):
    return lax.dot_general(left, right, NT, preferred_element_type=F32)


def one_hot_rows(low_row, count=WIDE):
    n = low_row.shape[1]
    rows = lax.broadcasted_iota(jnp.int32, (count, n), 0)
    return jnp.where(rows == low_row, 1.0, 0.0).astype(BF16)


def list_chunks(cnt_ref, list_ref, tiles_ref, buf_ref, sem_ref):
    def fetch(chunk):
        span = pl.ds(chunk * CHUNK, CHUNK)
        return pltpu.make_async_copy(tiles_ref.at[span], buf_ref.at[span], sem_ref.at[chunk])

    def block(b, total):
        chunks = (cnt_ref[0, b] + (CHUNK - 1)) >> 2
        for k in range(PER):
            list_ref[total + k] = b * PER + k

            @pl.when(k < chunks)
            def _():
                fetch(b * PER + k).start()

        return total + chunks

    total = lax.fori_loop(0, TB, block, jnp.int32(0))
    for u in range(UNROLL):
        list_ref[total + u] = 0

    def wait(step):
        def body(i, carry):
            fetch(list_ref[i]).wait()
            return carry

        first = step * UNROLL
        lax.fori_loop(first, jnp.minimum(first + UNROLL, total), body, 0)

    return total, wait


def chunk_slots(bid_ref, cnt_ref, list_ref, item, total):
    chunk = list_ref[item]
    block = chunk >> 2
    first = (chunk & (PER - 1)) * CHUNK
    count = jnp.where(item < total, cnt_ref[0, block], 0)
    slots = [(bid_ref[0, block, first + j], first + j < count) for j in range(CHUNK)]
    return chunk, block, slots


def place_marks(slot_ref, place_ref):
    slot = slot_ref[...]
    slot_lo = slot % WIDE
    for i in range(TGT // WIDE):
        span = slice(i * WIDE, (i + 1) * WIDE)
        place_ref[:, span] = one_hot_rows(slot_lo[:, span])
    return jnp.broadcast_to((slot // WIDE).astype(F32), (16, TGT)).astype(BF16)


def keep(values, high, wanted):
    mask = high == jnp.asarray(wanted, BF16)
    return [
        jnp.where(mask, values[r:r + 16], jnp.zeros((), BF16)) for r in range(0, values.shape[0], 16)
    ]


def forward_kernel(
    bid_ref, cnt_ref, feat_ref, tgt_ref, slot_ref, tiles_ref,
    out_ref, tgtq_ref,
    buf_ref, sem_ref, list_ref, place_ref, agg_ref,
):
    total, wait = list_chunks(cnt_ref, list_ref, tiles_ref, buf_ref, sem_ref)
    high16 = place_marks(slot_ref, place_ref)
    tgt = tgt_ref[...]
    row16 = lax.broadcasted_iota(jnp.int32, (16, TGT), 0)
    parts = jnp.where(row16 == 0, tgt // WIDE, jnp.where(row16 == 1, tgt % WIDE, 0)).astype(BF16)
    rows = []
    for q in range(TGT // WIDE):
        rows += keep(parts, high16, q)
    moved = dot_nt(jnp.concatenate(rows, axis=0), place_ref[...])
    for q in range(TGT // WIDE):
        tgtq_ref[:, q * WIDE:(q + 1) * WIDE] = moved[q * 16:q * 16 + 8]

    group = GROUP

    def gather(i, carry):
        span = pl.ds(pl.multiple_of(i * WIDE, WIDE), WIDE)
        ids = tgtq_ref[:, span]
        whole = (ids[0:1] * float(WIDE) + ids[1:2]).astype(jnp.int32)
        high = jnp.broadcast_to((whole // LOW).astype(F32), (8, WIDE))
        marks = one_hot_rows(whole % LOW, LOW)
        acc = [jnp.zeros((8, WIDE), F32) for _ in range(COLS // 8)]
        for g in range(NODES // LOW // group):
            left = jnp.concatenate(
                [
                    feat_ref[:, (g * group + n) * LOW:(g * group + n + 1) * LOW]
                    for n in range(group)
                ],
                axis=0,
            )
            prod = dot(left, marks)
            for n in range(group):
                mask = high == float(g * group + n)
                for c in range(COLS // 8):
                    at = n * COLS + c * 8
                    acc[c] = jnp.where(mask, prod[at:at + 8], acc[c])
        own = jnp.concatenate(acc, axis=0).astype(BF16)
        out_ref[2 * i, :COLS] = own[:, :BLK]
        out_ref[2 * i + 1, :COLS] = own[:, BLK:]
        return carry

    lax.fori_loop(0, TGT // WIDE, gather, 0, unroll=2)

    agg_ref[...] = jnp.zeros_like(agg_ref)

    def aggregate(i, carry):
        wait(i)
        done = []
        for u in range(UNROLL):
            chunk, block, slots = chunk_slots(bid_ref, cnt_ref, list_ref, i * UNROLL + u, total)
            left = []
            for node_block, live in slots:
                span = pl.ds(pl.multiple_of(node_block * BLK, BLK), BLK)
                left.append(jnp.where(live, feat_ref[:, span], jnp.zeros((), BF16)))
            tiles = buf_ref[pl.ds(chunk * CHUNK, CHUNK)].reshape(CHUNK * BLK, BLK)
            done.append((block, dot(jnp.concatenate(left, axis=1), tiles)))
        for block, prod in done:
            span = pl.ds(pl.multiple_of(block * BLK, BLK), BLK)
            agg_ref[:, span] += prod
        return carry

    lax.fori_loop(0, (total + UNROLL - 1) >> 4, aggregate, 0)

    aggregate_rows = agg_ref[...].astype(BF16)
    half = 8
    for g in range(TGT // WIDE // half):
        rows = []
        for q in range(half):
            rows += keep(aggregate_rows, high16, g * half + q)
        moved = dot_nt(jnp.concatenate(rows, axis=0), place_ref[...]).astype(BF16)
        for q in range(half):
            piece = moved[q * COLS:(q + 1) * COLS]
            out_ref[2 * (g * half + q), COLS:] = piece[:, :BLK]
            out_ref[2 * (g * half + q) + 1, COLS:] = piece[:, BLK:]


VMEM = pl.BlockSpec(memory_space=pltpu.VMEM)
SMEM = pl.BlockSpec(memory_space=pltpu.SMEM)


HBM = pl.BlockSpec(memory_space=pl.ANY)


def params(mib):
    return pltpu.CompilerParams(vmem_limit_bytes=mib * MIB)


def cost(microseconds):
    return pl.CostEstimate(
        flops=microseconds * 1100 * MIB,
        bytes_accessed=int(microseconds * 3.5 * MIB),
        transcendentals=0,
    )


BLOCKS = jax.ShapeDtypeStruct((FEAT, 2 * COLS, BLK), BF16)
TILE_BUFFER = [
    pltpu.VMEM((TB * MAXB, BLK, BLK), BF16),
    pltpu.SemaphoreType.DMA((TB * PER,)),
    pltpu.SMEM((LIST,), jnp.int32),
]


def forward(block_ids, counts, features, targets, slots, tiles):
    return pl.pallas_call(
        forward_kernel,
        out_shape=(
            BLOCKS,
            jax.ShapeDtypeStruct((8, TGT), F32),
        ),
        in_specs=[SMEM, SMEM, VMEM, VMEM, VMEM, HBM],
        out_specs=(VMEM, VMEM),
        scratch_shapes=TILE_BUFFER
        + [pltpu.VMEM((WIDE, TGT), BF16), pltpu.VMEM((COLS, TGT), F32)],
        compiler_params=params(40),
        cost_estimate=cost(15),
        name="gather_and_aggregate",
    )(block_ids, counts, features, targets, slots, tiles)


def middle_kernel(
    x_ref, w_ref, bias_ref, grad_ref, hidden_ref, back_ref, slope_ref
):
    half = FEAT * COLS
    x_own = x_ref[:, :COLS].reshape(half, BLK)
    x_agg = x_ref[:, COLS:].reshape(half, BLK)
    w_own = w_ref[:, :COLS].reshape(half, WIDE)
    w_agg = w_ref[:, COLS:].reshape(half, WIDE)
    tn = (((0,), (0,)), ((), ()))
    preact = lax.dot_general(x_own, w_own, tn, preferred_element_type=F32)
    preact = preact + lax.dot_general(x_agg, w_agg, tn, preferred_element_type=F32)
    preact = preact + bias_ref[...]
    sig = jax.nn.sigmoid(preact)
    hidden_ref[0] = (preact * sig).astype(BF16)
    slope = (grad_ref[0].astype(F32) * sig * (1.0 + preact * (1.0 - sig))).astype(BF16)
    back_ref[:, :COLS] = dot_nt(w_own, slope).astype(BF16).reshape(FEAT, COLS, BLK)
    back_ref[:, COLS:] = dot_nt(w_agg, slope).astype(BF16).reshape(FEAT, COLS, BLK)
    slope_ref[...] = slope


def weight_kernel(x_ref, slope_ref, wgrad_ref):
    half = FEAT * COLS
    slope = slope_ref[...]
    x_own = x_ref[:, :COLS].reshape(half, BLK)
    x_agg = x_ref[:, COLS:].reshape(half, BLK)
    wgrad_ref[:, :COLS] = dot(x_own, slope).astype(BF16).reshape(FEAT, COLS, WIDE)
    wgrad_ref[:, COLS:2 * COLS] = dot(x_agg, slope).astype(BF16).reshape(FEAT, COLS, WIDE)
    total = jnp.sum(slope.astype(F32), axis=0, keepdims=True)
    first = total.astype(BF16).astype(F32)
    rest = total - first
    second = rest.astype(BF16).astype(F32)
    third = rest - second
    row = lax.broadcasted_iota(jnp.int32, (16, WIDE), 0)
    tail = jnp.where(
        row == 0, first, jnp.where(row == 1, second, jnp.where(row == 2, third, 0.0))
    ).astype(BF16)
    wgrad_ref[:, 2 * COLS:] = jnp.broadcast_to(tail[None], (FEAT, 16, WIDE))


def weight_part(x, slope):
    return pl.pallas_call(
        weight_kernel,
        out_shape=jax.ShapeDtypeStruct((FEAT, 2 * COLS + 16, WIDE), BF16),
        in_specs=[VMEM] * 2,
        out_specs=VMEM,
        compiler_params=params(24),
        cost_estimate=cost(2),
        name="weight_partials",
    )(x, slope)


def middle(x, w, bias, grad):
    return pl.pallas_call(
        middle_kernel,
        out_shape=(
            jax.ShapeDtypeStruct((1, BLK, WIDE), BF16),
            BLOCKS,
            jax.ShapeDtypeStruct((BLK, WIDE), BF16),
        ),
        in_specs=[VMEM] * 4,
        out_specs=(VMEM,) * 3,
        compiler_params=params(24),
        cost_estimate=cost(2),
        name="hidden_and_slope",
    )(x, w, bias, grad)


def spread_kernel(
    bid_ref, cnt_ref, back_ref, slot_ref, tiles_ref, grad_ref, buf_ref, sem_ref, list_ref, rows_ref
):
    total, wait = list_chunks(cnt_ref, list_ref, tiles_ref, buf_ref, sem_ref)
    slot = slot_ref[...]
    slot_hi = (slot // WIDE).astype(F32)
    slot_lo = slot % WIDE
    pairs = TGT // WIDE
    left = jnp.concatenate(
        [jnp.concatenate([back_ref[2 * q, COLS:], back_ref[2 * q + 1, COLS:]], axis=1) for q in range(pairs)],
        axis=0,
    )
    for i in range(TGT // WIDE):
        span = slice(i * WIDE, (i + 1) * WIDE)
        prod = dot(left, one_hot_rows(slot_lo[:, span]))
        high = jnp.broadcast_to(slot_hi[:, span], (8, WIDE))
        acc = [jnp.zeros((8, WIDE), F32) for _ in range(COLS // 8)]
        for q in range(pairs):
            mask = high == float(q)
            for c in range(COLS // 8):
                at = q * COLS + c * 8
                acc[c] = jnp.where(mask, prod[at:at + 8], acc[c])
        rows_ref[:, span] = jnp.concatenate(acc, axis=0).astype(BF16)

    grad_ref[...] = jnp.zeros_like(grad_ref)

    def spread(i, carry):
        wait(i)
        done = []
        for u in range(UNROLL):
            chunk, block, slots = chunk_slots(bid_ref, cnt_ref, list_ref, i * UNROLL + u, total)
            span = pl.ds(pl.multiple_of(block * BLK, BLK), BLK)
            tiles = buf_ref[pl.ds(chunk * CHUNK, CHUNK)].reshape(CHUNK * BLK, BLK)
            done.append((slots, dot_nt(rows_ref[:, span], tiles)))
        for slots, prod in done:
            for j, (node_block, live) in enumerate(slots):
                piece = prod[:, j * BLK:(j + 1) * BLK]
                span = pl.ds(pl.multiple_of(node_block * BLK, BLK), BLK)
                grad_ref[:, span] += jnp.where(live, piece, 0.0)
        return carry

    lax.fori_loop(0, (total + UNROLL - 1) >> 4, spread, 0)


def spread_part(block_ids, counts, back, slots, tiles):
    return pl.pallas_call(
        spread_kernel,
        out_shape=jax.ShapeDtypeStruct((COLS, NODES), F32),
        in_specs=[SMEM, SMEM, VMEM, VMEM, HBM],
        out_specs=VMEM,
        scratch_shapes=TILE_BUFFER + [pltpu.VMEM((COLS, TGT), BF16)],
        compiler_params=params(40),
        cost_estimate=cost(7),
        name="spread",
    )(block_ids, counts, back, slots, tiles)


QUARTER = NODES // 4


def scatter_kernel(zid_ref, grad_ref, back_ref, tgtq_ref, *refs, steps, plus):
    extra_refs, out_refs, mark_ref = refs[:plus], refs[plus:-1], refs[-1]
    ids = tgtq_ref[...]
    for i in range(TGT // WIDE):
        span = slice(i * WIDE, (i + 1) * WIDE)
        mark_ref[:, span] = one_hot_rows(ids[1:2, span].astype(jnp.int32))
    high16 = jnp.broadcast_to(ids[0:1], (16, TGT)).astype(BF16)
    own = jnp.concatenate([back_ref[q, :COLS] for q in range(FEAT)], axis=1)
    per = QUARTER // WIDE
    half = 8
    for step, out_ref in zip(steps, out_refs):
        which = (zid_ref[0] + step) & 3
        for g in range(per // half):
            rows = []
            for n in range(half):
                wanted = (which * per + g * half + n).astype(F32).astype(BF16)
                rows += keep(own, high16, wanted)
            prod = dot_nt(jnp.concatenate(rows, axis=0), mark_ref[...])
            for n in range(half):
                at = (g * half + n) * WIDE
                span = pl.ds(pl.multiple_of(which * QUARTER + at, WIDE), WIDE)
                value = grad_ref[:, span] + prod[n * COLS:(n + 1) * COLS]
                for ref in extra_refs:
                    value = value + ref[:, at:at + WIDE].astype(F32)
                out_ref[:, at:at + WIDE] = value.astype(out_ref.dtype)


def scatter_part(zid, grad, back, tgtq, steps, *extra):
    return pl.pallas_call(
        lambda *refs: scatter_kernel(*refs, steps=steps, plus=len(extra)),
        out_shape=tuple(
            jax.ShapeDtypeStruct((COLS, QUARTER), BF16 if step else F32) for step in steps
        ),
        in_specs=[SMEM] + [VMEM] * (3 + len(extra)),
        out_specs=tuple(VMEM for _ in steps),
        scratch_shapes=[pltpu.VMEM((WIDE, TGT), BF16)],
        compiler_params=params(24),
        cost_estimate=cost(15 if extra else 1 + len(steps)),
        name="scatter",
    )(zid, grad, back, tgtq, *extra)


def place_kernel(zid_ref, *refs, steps, fresh):
    parts = refs[:len(steps)]
    out_ref, wide_ref, sem = refs[len(steps) + (0 if fresh else 1):]
    copies = []
    for k, (step, ref) in enumerate(zip(steps, parts)):
        at = pl.multiple_of(((zid_ref[0] + step) & 3) * QUARTER, QUARTER)
        wide_ref[k] = ref[...].astype(F32)
        copies.append(
            pltpu.make_async_copy(wide_ref.at[k], out_ref.at[:, pl.ds(at, QUARTER)], sem.at[k])
        )
        copies[-1].start()
    for copy in copies:
        copy.wait()


def place(zid, parts, steps, whole=None):
    count, fresh = len(steps), whole is None
    return pl.pallas_call(
        lambda *refs: place_kernel(*refs, steps=steps, fresh=fresh),
        out_shape=jax.ShapeDtypeStruct((COLS, NODES), F32),
        in_specs=[SMEM] + [VMEM] * count + ([] if fresh else [HBM]),
        out_specs=HBM,
        scratch_shapes=[
            pltpu.VMEM((count, COLS, QUARTER), F32),
            pltpu.SemaphoreType.DMA((count,)),
        ],
        input_output_aliases={} if fresh else {1 + count: 0},
        compiler_params=params(24),
        cost_estimate=cost(1),
        name="place_quarters",
    )(zid, *parts, *(() if fresh else (whole,)))


def shift(value, by):
    return lax.ppermute(value, "dp", [(k, (k + by) % 4) for k in range(4)])


def exchange(value):
    return lax.all_to_all(value, "feat", 0, 0, tiled=True)


def shards(
    features,
    targets,
    block_ids,
    counts,
    target_slots,
    edge_tiles,
    self_weight,
    neigh_weight,
    hidden_bias,
    hidden_grad,
):
    tiles = edge_tiles.reshape(TB * MAXB, BLK, BLK)
    zid = lax.axis_index("dp").astype(jnp.int32).reshape(1)

    side = lax.axis_index("feat") % 2

    weights = jnp.concatenate([self_weight, neigh_weight], axis=0)
    weights = exchange(jnp.broadcast_to(weights[None], (FEAT, 2 * COLS, WIDE)))
    sent, tgtq = forward(block_ids, counts, features, targets, target_slots, tiles)
    sent, weights = lax.optimization_barrier((sent, weights))
    got = exchange(sent)
    hidden, back, slope = middle(got, weights, hidden_bias.reshape(1, -1), hidden_grad)
    back = exchange(back)
    wgrad = weight_part(got, slope)
    back, wgrad = lax.optimization_barrier((back, wgrad))
    wgrad = exchange(wgrad)
    grad = spread_part(block_ids, counts, back, target_slots, tiles)
    (far2,) = scatter_part(zid, grad, back, tgtq, (2,))
    grad, far2 = lax.optimization_barrier((grad, far2))
    from_far = shift(far2, 2)
    far1, far3 = scatter_part(zid, grad, back, tgtq, (1, 3))
    from_last, from_next = shift(far1, 1), shift(far3, 3)
    (near,) = scatter_part(zid, grad, back, tgtq, (0,), from_far)
    near, wgrad = lax.optimization_barrier((near, wgrad))

    wsum = jnp.sum(wgrad[:, :2 * COLS + 8].astype(F32), axis=0)
    wsum = (wsum + shift(wsum, 2)) + (shift(wsum, 1) + shift(wsum, 3))
    self_grad = wsum[:COLS]
    neigh_grad = wsum[COLS:2 * COLS]
    bias_grad = wsum[2 * COLS] + (wsum[2 * COLS + 1] + wsum[2 * COLS + 2])

    done = near + from_last.astype(F32) + from_next.astype(F32)
    done = done.astype(BF16)
    of_far, of_next, of_last = shift(done, 2), shift(done, 3), shift(done, 1)
    feature_grad = place(zid, (done, of_far), (0, 2))
    feature_grad = place(zid, (of_next, of_last), (1, 3), feature_grad)
    return (hidden, feature_grad, self_grad, neigh_grad, bias_grad)


def solution(mesh):
    return jax.shard_map(
        shards,
        mesh=mesh,
        in_specs=(
            P("feat", None),
            P("dp", None),
            P("dp", None, None),
            P("dp", None),
            P("dp", None),
            P("dp", None, None, None, None),
            P("feat", None),
            P("feat", None),
            P(),
            P("dp", "feat", None),
        ),
        out_specs=(P("dp", "feat", None), P("feat", None), P("feat", None), P("feat", None), P()),
        check_vma=False,
    )
```

```python
import jax
import jax.numpy as jnp
from jax import lax
from jax.experimental import pallas as pl
from jax.experimental.pallas import tpu as pltpu
from jax.sharding import PartitionSpec as P

BLK = 128
MAXB = 16
TB = 32
NBLK = 128
TGT = 4096
NODES = 16384
COLS = 32
FEAT = 32
WIDE = 256
CHUNK = 2
PER = MAXB // CHUNK
UNROLL = 32
LOW = 512
GROUP = 32
LIST = TB * PER + UNROLL
MIB = 1024 * 1024

F32 = jnp.float32
BF16 = jnp.bfloat16
NT = (((1,), (1,)), ((), ()))


def dot(left, right):
    return jnp.dot(left, right, preferred_element_type=F32)


def dot_nt(left, right):
    return lax.dot_general(left, right, NT, preferred_element_type=F32)


def one_hot_rows(low_row, count=WIDE):
    n = low_row.shape[1]
    rows = lax.broadcasted_iota(jnp.int32, (count, n), 0)
    return jnp.where(rows == low_row, 1.0, 0.0).astype(BF16)


def list_chunks(cnt_ref, list_ref, tiles_ref, buf_ref, sem_ref):
    def fetch(chunk):
        span = pl.ds(chunk * CHUNK, CHUNK)
        return pltpu.make_async_copy(tiles_ref.at[span], buf_ref.at[span], sem_ref.at[chunk])

    def block(b, total):
        chunks = (cnt_ref[0, b] + (CHUNK - 1)) >> 1
        for k in range(PER):
            list_ref[total + k] = b * PER + k

            @pl.when(k < chunks)
            def _():
                fetch(b * PER + k).start()

        return total + chunks

    total = lax.fori_loop(0, TB, block, jnp.int32(0))
    for u in range(UNROLL):
        list_ref[total + u] = 0

    def wait(step):
        def body(i, carry):
            fetch(list_ref[i]).wait()
            return carry

        first = step * UNROLL
        lax.fori_loop(first, jnp.minimum(first + UNROLL, total), body, 0)

    return total, wait


def chunk_slots(bid_ref, cnt_ref, list_ref, item, total):
    chunk = list_ref[item]
    block = chunk >> 3
    first = (chunk & (PER - 1)) * CHUNK
    count = jnp.where(item < total, cnt_ref[0, block], 0)
    slots = [(bid_ref[0, block, first + j], first + j < count) for j in range(CHUNK)]
    return chunk, block, slots


def place_marks(slot_ref, place_ref):
    slot = slot_ref[...]
    slot_lo = slot % WIDE
    for i in range(TGT // WIDE):
        span = slice(i * WIDE, (i + 1) * WIDE)
        place_ref[:, span] = one_hot_rows(slot_lo[:, span])
    return jnp.broadcast_to((slot // WIDE).astype(F32), (16, TGT)).astype(BF16)


def keep(values, high, wanted):
    mask = high == jnp.asarray(wanted, BF16)
    return [
        jnp.where(mask, values[r:r + 16], jnp.zeros((), BF16)) for r in range(0, values.shape[0], 16)
    ]


def forward_kernel(
    bid_ref, cnt_ref, feat_ref, tgt_ref, slot_ref, tiles_ref,
    out_ref, tgtq_ref,
    buf_ref, sem_ref, list_ref, place_ref, agg_ref,
):
    total, wait = list_chunks(cnt_ref, list_ref, tiles_ref, buf_ref, sem_ref)
    high16 = place_marks(slot_ref, place_ref)
    tgt = tgt_ref[...]
    row16 = lax.broadcasted_iota(jnp.int32, (16, TGT), 0)
    parts = jnp.where(row16 == 0, tgt // WIDE, jnp.where(row16 == 1, tgt % WIDE, 0)).astype(BF16)
    rows = []
    for q in range(TGT // WIDE):
        rows += keep(parts, high16, q)
    moved = dot_nt(jnp.concatenate(rows, axis=0), place_ref[...])
    for q in range(TGT // WIDE):
        tgtq_ref[:, q * WIDE:(q + 1) * WIDE] = moved[q * 16:q * 16 + 8]

    group = GROUP

    def gather(i, carry):
        span = pl.ds(pl.multiple_of(i * WIDE, WIDE), WIDE)
        ids = tgtq_ref[:, span]
        whole = (ids[0:1] * float(WIDE) + ids[1:2]).astype(jnp.int32)
        high = jnp.broadcast_to((whole // LOW).astype(F32), (8, WIDE))
        marks = one_hot_rows(whole % LOW, LOW)
        acc = [jnp.zeros((8, WIDE), F32) for _ in range(COLS // 8)]
        for g in range(NODES // LOW // group):
            left = jnp.concatenate(
                [
                    feat_ref[:, (g * group + n) * LOW:(g * group + n + 1) * LOW]
                    for n in range(group)
                ],
                axis=0,
            )
            prod = dot(left, marks)
            for n in range(group):
                mask = high == float(g * group + n)
                for c in range(COLS // 8):
                    at = n * COLS + c * 8
                    acc[c] = jnp.where(mask, prod[at:at + 8], acc[c])
        own = jnp.concatenate(acc, axis=0).astype(BF16)
        out_ref[2 * i, :COLS] = own[:, :BLK]
        out_ref[2 * i + 1, :COLS] = own[:, BLK:]
        return carry

    lax.fori_loop(0, TGT // WIDE, gather, 0, unroll=2)

    agg_ref[...] = jnp.zeros_like(agg_ref)

    def aggregate(i, carry):
        wait(i)
        done = []
        for u in range(UNROLL):
            chunk, block, slots = chunk_slots(bid_ref, cnt_ref, list_ref, i * UNROLL + u, total)
            left = []
            for node_block, live in slots:
                span = pl.ds(pl.multiple_of(node_block * BLK, BLK), BLK)
                left.append(jnp.where(live, feat_ref[:, span], jnp.zeros((), BF16)))
            tiles = buf_ref[pl.ds(chunk * CHUNK, CHUNK)].reshape(CHUNK * BLK, BLK)
            done.append((block, dot(jnp.concatenate(left, axis=1), tiles)))
        for block, prod in done:
            span = pl.ds(pl.multiple_of(block * BLK, BLK), BLK)
            agg_ref[:, span] += prod
        return carry

    lax.fori_loop(0, (total + UNROLL - 1) >> 5, aggregate, 0)

    aggregate_rows = agg_ref[...].astype(BF16)
    half = 8
    for g in range(TGT // WIDE // half):
        rows = []
        for q in range(half):
            rows += keep(aggregate_rows, high16, g * half + q)
        moved = dot_nt(jnp.concatenate(rows, axis=0), place_ref[...]).astype(BF16)
        for q in range(half):
            piece = moved[q * COLS:(q + 1) * COLS]
            out_ref[2 * (g * half + q), COLS:] = piece[:, :BLK]
            out_ref[2 * (g * half + q) + 1, COLS:] = piece[:, BLK:]


VMEM = pl.BlockSpec(memory_space=pltpu.VMEM)
SMEM = pl.BlockSpec(memory_space=pltpu.SMEM)


HBM = pl.BlockSpec(memory_space=pl.ANY)


def params(mib):
    return pltpu.CompilerParams(vmem_limit_bytes=mib * MIB)


def cost(microseconds):
    return pl.CostEstimate(
        flops=microseconds * 1100 * MIB,
        bytes_accessed=int(microseconds * 3.5 * MIB),
        transcendentals=0,
    )


BLOCKS = jax.ShapeDtypeStruct((FEAT, 2 * COLS, BLK), BF16)
TILE_BUFFER = [
    pltpu.VMEM((TB * MAXB, BLK, BLK), BF16),
    pltpu.SemaphoreType.DMA((TB * PER,)),
    pltpu.SMEM((LIST,), jnp.int32),
]


def forward(block_ids, counts, features, targets, slots, tiles):
    return pl.pallas_call(
        forward_kernel,
        out_shape=(
            BLOCKS,
            jax.ShapeDtypeStruct((8, TGT), F32),
        ),
        in_specs=[SMEM, SMEM, VMEM, VMEM, VMEM, HBM],
        out_specs=(VMEM, VMEM),
        scratch_shapes=TILE_BUFFER
        + [pltpu.VMEM((WIDE, TGT), BF16), pltpu.VMEM((COLS, TGT), F32)],
        compiler_params=params(40),
        cost_estimate=cost(15),
        name="gather_and_aggregate",
    )(block_ids, counts, features, targets, slots, tiles)


def middle_kernel(
    x_ref, w_ref, bias_ref, grad_ref, hidden_ref, back_ref, slope_ref
):
    half = FEAT * COLS
    x_own = x_ref[:, :COLS].reshape(half, BLK)
    x_agg = x_ref[:, COLS:].reshape(half, BLK)
    w_own = w_ref[:, :COLS].reshape(half, WIDE)
    w_agg = w_ref[:, COLS:].reshape(half, WIDE)
    tn = (((0,), (0,)), ((), ()))
    preact = lax.dot_general(x_own, w_own, tn, preferred_element_type=F32)
    preact = preact + lax.dot_general(x_agg, w_agg, tn, preferred_element_type=F32)
    preact = preact + bias_ref[...]
    sig = jax.nn.sigmoid(preact)
    hidden_ref[0] = (preact * sig).astype(BF16)
    slope = (grad_ref[0].astype(F32) * sig * (1.0 + preact * (1.0 - sig))).astype(BF16)
    back_ref[:, :COLS] = dot_nt(w_own, slope).astype(BF16).reshape(FEAT, COLS, BLK)
    back_ref[:, COLS:] = dot_nt(w_agg, slope).astype(BF16).reshape(FEAT, COLS, BLK)
    slope_ref[...] = slope


def weight_kernel(x_ref, slope_ref, wgrad_ref):
    half = FEAT * COLS
    slope = slope_ref[...]
    x_own = x_ref[:, :COLS].reshape(half, BLK)
    x_agg = x_ref[:, COLS:].reshape(half, BLK)
    wgrad_ref[:, :COLS] = dot(x_own, slope).astype(BF16).reshape(FEAT, COLS, WIDE)
    wgrad_ref[:, COLS:2 * COLS] = dot(x_agg, slope).astype(BF16).reshape(FEAT, COLS, WIDE)
    total = jnp.sum(slope.astype(F32), axis=0, keepdims=True)
    first = total.astype(BF16).astype(F32)
    rest = total - first
    second = rest.astype(BF16).astype(F32)
    third = rest - second
    row = lax.broadcasted_iota(jnp.int32, (16, WIDE), 0)
    tail = jnp.where(
        row == 0, first, jnp.where(row == 1, second, jnp.where(row == 2, third, 0.0))
    ).astype(BF16)
    wgrad_ref[:, 2 * COLS:] = jnp.broadcast_to(tail[None], (FEAT, 16, WIDE))


def weight_part(x, slope):
    return pl.pallas_call(
        weight_kernel,
        out_shape=jax.ShapeDtypeStruct((FEAT, 2 * COLS + 16, WIDE), BF16),
        in_specs=[VMEM] * 2,
        out_specs=VMEM,
        compiler_params=params(24),
        cost_estimate=cost(2),
        name="weight_partials",
    )(x, slope)


def middle(x, w, bias, grad):
    return pl.pallas_call(
        middle_kernel,
        out_shape=(
            jax.ShapeDtypeStruct((1, BLK, WIDE), BF16),
            BLOCKS,
            jax.ShapeDtypeStruct((BLK, WIDE), BF16),
        ),
        in_specs=[VMEM] * 4,
        out_specs=(VMEM,) * 3,
        compiler_params=params(24),
        cost_estimate=cost(2),
        name="hidden_and_slope",
    )(x, w, bias, grad)


def spread_kernel(
    bid_ref, cnt_ref, back_ref, slot_ref, tiles_ref, grad_ref, buf_ref, sem_ref, list_ref, rows_ref
):
    total, wait = list_chunks(cnt_ref, list_ref, tiles_ref, buf_ref, sem_ref)
    slot = slot_ref[...]
    slot_hi = (slot // WIDE).astype(F32)
    slot_lo = slot % WIDE
    pairs = TGT // WIDE
    left = jnp.concatenate(
        [jnp.concatenate([back_ref[2 * q, COLS:], back_ref[2 * q + 1, COLS:]], axis=1) for q in range(pairs)],
        axis=0,
    )
    for i in range(TGT // WIDE):
        span = slice(i * WIDE, (i + 1) * WIDE)
        prod = dot(left, one_hot_rows(slot_lo[:, span]))
        high = jnp.broadcast_to(slot_hi[:, span], (8, WIDE))
        acc = [jnp.zeros((8, WIDE), F32) for _ in range(COLS // 8)]
        for q in range(pairs):
            mask = high == float(q)
            for c in range(COLS // 8):
                at = q * COLS + c * 8
                acc[c] = jnp.where(mask, prod[at:at + 8], acc[c])
        rows_ref[:, span] = jnp.concatenate(acc, axis=0).astype(BF16)

    grad_ref[...] = jnp.zeros_like(grad_ref)

    def spread(i, carry):
        wait(i)
        done = []
        for u in range(UNROLL):
            chunk, block, slots = chunk_slots(bid_ref, cnt_ref, list_ref, i * UNROLL + u, total)
            span = pl.ds(pl.multiple_of(block * BLK, BLK), BLK)
            tiles = buf_ref[pl.ds(chunk * CHUNK, CHUNK)].reshape(CHUNK * BLK, BLK)
            done.append((slots, dot_nt(rows_ref[:, span], tiles)))
        for slots, prod in done:
            for j, (node_block, live) in enumerate(slots):
                piece = prod[:, j * BLK:(j + 1) * BLK]
                span = pl.ds(pl.multiple_of(node_block * BLK, BLK), BLK)
                grad_ref[:, span] += jnp.where(live, piece, 0.0)
        return carry

    lax.fori_loop(0, (total + UNROLL - 1) >> 5, spread, 0)


def spread_part(block_ids, counts, back, slots, tiles):
    return pl.pallas_call(
        spread_kernel,
        out_shape=jax.ShapeDtypeStruct((COLS, NODES), F32),
        in_specs=[SMEM, SMEM, VMEM, VMEM, HBM],
        out_specs=VMEM,
        scratch_shapes=TILE_BUFFER + [pltpu.VMEM((COLS, TGT), BF16)],
        compiler_params=params(40),
        cost_estimate=cost(7),
        name="spread",
    )(block_ids, counts, back, slots, tiles)


QUARTER = NODES // 4


def scatter_kernel(zid_ref, grad_ref, back_ref, tgtq_ref, *refs, steps, plus):
    extra_refs, out_refs, mark_ref = refs[:plus], refs[plus:-1], refs[-1]
    ids = tgtq_ref[...]
    for i in range(TGT // WIDE):
        span = slice(i * WIDE, (i + 1) * WIDE)
        mark_ref[:, span] = one_hot_rows(ids[1:2, span].astype(jnp.int32))
    high16 = jnp.broadcast_to(ids[0:1], (16, TGT)).astype(BF16)
    own = jnp.concatenate([back_ref[q, :COLS] for q in range(FEAT)], axis=1)
    per = QUARTER // WIDE
    half = 8
    for step, out_ref in zip(steps, out_refs):
        which = (zid_ref[0] + step) & 3
        for g in range(per // half):
            rows = []
            for n in range(half):
                wanted = (which * per + g * half + n).astype(F32).astype(BF16)
                rows += keep(own, high16, wanted)
            prod = dot_nt(jnp.concatenate(rows, axis=0), mark_ref[...])
            for n in range(half):
                at = (g * half + n) * WIDE
                span = pl.ds(pl.multiple_of(which * QUARTER + at, WIDE), WIDE)
                value = grad_ref[:, span] + prod[n * COLS:(n + 1) * COLS]
                for ref in extra_refs:
                    value = value + ref[:, at:at + WIDE].astype(F32)
                out_ref[:, at:at + WIDE] = value.astype(out_ref.dtype)


def scatter_part(zid, grad, back, tgtq, steps, *extra):
    return pl.pallas_call(
        lambda *refs: scatter_kernel(*refs, steps=steps, plus=len(extra)),
        out_shape=tuple(
            jax.ShapeDtypeStruct((COLS, QUARTER), BF16 if step else F32) for step in steps
        ),
        in_specs=[SMEM] + [VMEM] * (3 + len(extra)),
        out_specs=tuple(VMEM for _ in steps),
        scratch_shapes=[pltpu.VMEM((WIDE, TGT), BF16)],
        compiler_params=params(24),
        cost_estimate=cost(15 if extra else 1 + len(steps)),
        name="scatter",
    )(zid, grad, back, tgtq, *extra)


def place_kernel(zid_ref, *refs, steps, fresh):
    parts = refs[:len(steps)]
    out_ref, wide_ref, sem = refs[len(steps) + (0 if fresh else 1):]
    copies = []
    for k, (step, ref) in enumerate(zip(steps, parts)):
        at = pl.multiple_of(((zid_ref[0] + step) & 3) * QUARTER, QUARTER)
        wide_ref[k] = ref[...].astype(F32)
        copies.append(
            pltpu.make_async_copy(wide_ref.at[k], out_ref.at[:, pl.ds(at, QUARTER)], sem.at[k])
        )
        copies[-1].start()
    for copy in copies:
        copy.wait()


def place(zid, parts, steps, whole=None):
    count, fresh = len(steps), whole is None
    return pl.pallas_call(
        lambda *refs: place_kernel(*refs, steps=steps, fresh=fresh),
        out_shape=jax.ShapeDtypeStruct((COLS, NODES), F32),
        in_specs=[SMEM] + [VMEM] * count + ([] if fresh else [HBM]),
        out_specs=HBM,
        scratch_shapes=[
            pltpu.VMEM((count, COLS, QUARTER), F32),
            pltpu.SemaphoreType.DMA((count,)),
        ],
        input_output_aliases={} if fresh else {1 + count: 0},
        compiler_params=params(24),
        cost_estimate=cost(1),
        name="place_quarters",
    )(zid, *parts, *(() if fresh else (whole,)))


def shift(value, by):
    return lax.ppermute(value, "dp", [(k, (k + by) % 4) for k in range(4)])


def exchange(value):
    return lax.all_to_all(value, "feat", 0, 0, tiled=True)


def shards(
    features,
    targets,
    block_ids,
    counts,
    target_slots,
    edge_tiles,
    self_weight,
    neigh_weight,
    hidden_bias,
    hidden_grad,
):
    tiles = edge_tiles.reshape(TB * MAXB, BLK, BLK)
    zid = lax.axis_index("dp").astype(jnp.int32).reshape(1)

    side = lax.axis_index("feat") % 2

    weights = jnp.concatenate([self_weight, neigh_weight], axis=0)
    weights = exchange(jnp.broadcast_to(weights[None], (FEAT, 2 * COLS, WIDE)))
    sent, tgtq = forward(block_ids, counts, features, targets, target_slots, tiles)
    sent, weights = lax.optimization_barrier((sent, weights))
    got = exchange(sent)
    hidden, back, slope = middle(got, weights, hidden_bias.reshape(1, -1), hidden_grad)
    back = exchange(back)
    wgrad = weight_part(got, slope)
    back, wgrad = lax.optimization_barrier((back, wgrad))
    wgrad = exchange(wgrad)
    grad = spread_part(block_ids, counts, back, target_slots, tiles)
    (far2,) = scatter_part(zid, grad, back, tgtq, (2,))
    grad, far2 = lax.optimization_barrier((grad, far2))
    from_far = shift(far2, 2)
    far1, far3 = scatter_part(zid, grad, back, tgtq, (1, 3))
    from_last, from_next = shift(far1, 1), shift(far3, 3)
    (near,) = scatter_part(zid, grad, back, tgtq, (0,), from_far)
    near, wgrad = lax.optimization_barrier((near, wgrad))

    wsum = jnp.sum(wgrad[:, :2 * COLS + 8].astype(F32), axis=0)
    wsum = (wsum + shift(wsum, 2)) + (shift(wsum, 1) + shift(wsum, 3))
    self_grad = wsum[:COLS]
    neigh_grad = wsum[COLS:2 * COLS]
    bias_grad = wsum[2 * COLS] + (wsum[2 * COLS + 1] + wsum[2 * COLS + 2])

    done = near + from_last.astype(F32) + from_next.astype(F32)
    done = done.astype(BF16)
    of_far, of_next, of_last = shift(done, 2), shift(done, 3), shift(done, 1)
    feature_grad = place(zid, (done, of_far), (0, 2))
    feature_grad = place(zid, (of_next, of_last), (1, 3), feature_grad)
    return (hidden, feature_grad, self_grad, neigh_grad, bias_grad)


def solution(mesh):
    return jax.shard_map(
        shards,
        mesh=mesh,
        in_specs=(
            P("feat", None),
            P("dp", None),
            P("dp", None, None),
            P("dp", None),
            P("dp", None),
            P("dp", None, None, None, None),
            P("feat", None),
            P("feat", None),
            P(),
            P("dp", "feat", None),
        ),
        out_specs=(P("dp", "feat", None), P("feat", None), P("feat", None), P("feat", None), P()),
        check_vma=False,
    )
```
